768 devices in a mesh: lon: 24 (over z, y_hi), lat: 32 (over x, y_lo, core).
Axes of the slice: x: 4, y: 8 (y_hi: 2, y_lo: 4; y = y_hi * 4 + y_lo), z: 12, core: 2. Of those that a mesh axis runs over, the one named last changes fastest.
Arguments:
- tracers: float32 [3, 8, 256, 3072], P(None, None, 'lat', 'lon'), may hold values from -6 to 6
- cotangent: float32 [3, 8, 256, 3072], P(None, None, 'lat', 'lon'), may hold values from -6 to 6
- east_vel: float32 [8, 256, 3072], P(None, 'lat', 'lon'), may hold values from -0.3 to 0.3
- north_vel: float32 [8, 256, 3072], P(None, 'lat', 'lon'), may hold values from -0.3 to 0.3
- sea_mask: int32 [256, 3072], P('lat', 'lon'), may hold values 0 or 1
- level_count: int32 [256, 3072], P('lat', 'lon'), may hold values from 1 to 8
Outputs:
- adj_tracers: float32 [3, 8, 256, 3072], P(None, None, 'lat', 'lon')
- adj_east: float32 [8, 256, 3072], P(None, 'lat', 'lon')
- adj_north: float32 [8, 256, 3072], P(None, 'lat', 'lon')
The draws below stay inside these ranges and needn't reach their ends.
All inputs are finite; a program needn't handle non-finite values. No bound on the sum of `sea_mask` on one device may be relied on, other than what follows from the above.
Results may differ from the reference program's by a relative error of at most 0.00002.
Values sent between devices are 32-bit elements; how exact they have to be, the bound alone decides.
A program may use at most 32 MiB of HBM per device.

```python
import jax
import jax.numpy as jnp
from jax import lax

TRACERS = 3
LEV = 8
STEPS = 4
NLAT = 256
NLON = 3072


def draw_cotangent(key, part):
    shape = (TRACERS, LEV, NLAT, NLON)
    own_key = jax.random.fold_in(key, 101)
    return jnp.clip(jax.random.normal(own_key, shape, jnp.float32), -6.0, 6.0)


def draw_east_vel(key, part):
    shape = (LEV, NLAT, NLON)
    own_key = jax.random.fold_in(key, 202)
    return jax.random.uniform(own_key, shape, jnp.float32, -0.3, 0.3)


def draw_north_vel(key, part):
    shape = (LEV, NLAT, NLON)
    own_key = jax.random.fold_in(key, 303)
    return jax.random.uniform(own_key, shape, jnp.float32, -0.3, 0.3)


def with_ends(drawn, rng, least, top_value):
    place = [jax.random.randint(jax.random.fold_in(rng, axis), (), 0, length) for axis, length in enumerate(drawn.shape)]
    main_axis = drawn.shape.index(max(drawn.shape))
    next_to = place[:main_axis] + [(place[main_axis] + 1) % drawn.shape[main_axis]] + place[main_axis + 1:]
    return drawn.at[tuple(place)].set(least).at[tuple(next_to)].set(top_value)


def shard_levels(rng, extent, shards, low, high):
    gain, own = 1.0, jax.random.fold_in(rng, 6)
    for dim, shards_of in shards:
        heights = jnp.exp(jax.random.uniform(jax.random.fold_in(own, dim), (shards_of,), jnp.float32, low / len(shards), high / len(shards)))
        gain = gain * jnp.repeat(heights, extent[dim] // shards_of).reshape([-1 if axis == dim else 1 for axis in range(len(extent))])
    return gain


def noise(stream_key, shape, deviation, reach, pieces=(), dtype=jnp.bfloat16):
    values = jax.random.normal(stream_key, shape, jnp.float32) * deviation
    if len(pieces) > 0:
        values = shard_levels(stream_key, shape, pieces, -0.22, 0.18) * values
    return jnp.clip(values, min=-reach, max=reach).astype(dtype)


def setup_inputs(seed: int = 0) -> dict:
    streams_of = jax.random.split(jax.random.key(seed), 7)
    return {
        "tracers": noise(streams_of[0], (TRACERS, LEV, NLAT, NLON), 1.0, 6.0, ((2, 32), (3, 24)), jnp.float32),
        "cotangent": draw_cotangent(jax.random.fold_in(streams_of[6], 71), 0),
        "east_vel": draw_east_vel(jax.random.fold_in(streams_of[6], 71), 0),
        "north_vel": draw_north_vel(jax.random.fold_in(streams_of[6], 71), 0),
        "sea_mask": with_ends((jax.random.randint(streams_of[4], (NLAT, NLON), 0, 8) < 7).astype(jnp.int32), jax.random.fold_in(streams_of[4], 1), 0, 1),
        "level_count": with_ends(jax.random.randint(streams_of[5], (NLAT, NLON), 1, LEV + 1), jax.random.fold_in(streams_of[5], 1), 1, LEV).astype(jnp.int32),
    }


horiz_diff = 0.22
vert_diff = 0.05

def advance(tracer, east_field, north_field, wetness):
    row_part = tracer[..., 1:-1, :]
    row_wet = wetness[:, 1:-1, :]
    east_open = row_wet[:, :, :-1] * row_wet[:, :, 1:]
    east_flux = east_open * (east_field[:, 1:-1, :-1] * 0.5 * (row_part[..., :-1] + row_part[..., 1:]) - horiz_diff * (row_part[..., 1:] - row_part[..., :-1]))
    column_part = tracer[..., :, 1:-1]
    column_wet = wetness[:, :, 1:-1]
    north_open = column_wet[:, :-1, :] * column_wet[:, 1:, :]
    north_flux = north_open * (north_field[:, :-1, 1:-1] * 0.5 * (column_part[..., :-1, :] + column_part[..., 1:, :]) - horiz_diff * (column_part[..., 1:, :] - column_part[..., :-1, :]))
    centre = tracer[..., 1:-1, 1:-1]
    centre_wet = wetness[:, 1:-1, 1:-1]
    vertical_open = centre_wet[:-1] * centre_wet[1:]
    vertical_flux = vertical_open * vert_diff * (centre[..., 1:, :, :] - centre[..., :-1, :, :])
    nothing = jnp.zeros_like(centre[..., :1, :, :])
    mixing = jnp.concatenate([vertical_flux, nothing], -3) - jnp.concatenate([nothing, vertical_flux], -3)
    return centre_wet * (centre - (east_flux[..., 1:] - east_flux[..., :-1]) - (north_flux[..., 1:, :] - north_flux[..., :-1, :]) + mixing)

def wet_cells(sea_mask, level_count):
    level_index = lax.broadcasted_iota(jnp.int32, (LEV,) + sea_mask.shape, 0)
    return jnp.where((sea_mask[None] == 1) & (level_index < level_count[None]), 1.0, 0.0).astype(jnp.float32)

def widen(field_in):
    wrapped = jnp.concatenate([field_in[..., -1:], field_in, field_in[..., :1]], -1)
    border = jnp.zeros_like(wrapped[..., :1, :])
    return jnp.concatenate([border, wrapped, border], -2)

def reference(tracers, cotangent, east_vel, north_vel, sea_mask, level_count):
    wide_wet = widen(wet_cells(sea_mask, level_count))

    def forward(initial, east_field, north_field):
        east_wide = widen(east_field)
        north_wide = widen(north_field)
        current = initial
        for repeat in range(STEPS):
            current = jax.checkpoint(advance)(widen(current), east_wide, north_wide, wide_wet)
        return current

    def one_tracer(members):
        initial, sensitivity = members
        ending, pullback = jax.vjp(forward, initial[None], east_vel, north_vel)
        gradients = pullback(sensitivity[None])
        return (gradients[0][0], gradients[1], gradients[2])
    adj_tracers, east_parts, north_parts = lax.map(one_tracer, (tracers, cotangent))
    return (adj_tracers, lax.optimization_barrier(jnp.sum(east_parts, 0)), lax.optimization_barrier(jnp.sum(north_parts, 0)))
```

```python
import jax
import jax.numpy as jnp
from jax import lax
from jax.experimental import pallas as pl
from jax.experimental.pallas import tpu as pltpu
from jax.sharding import PartitionSpec as P

MESH = pl.DeviceIdType.MESH
STEPS = 4
HALO = 4
HORIZ = 0.22
VERT = 0.05

TRACER, COTAN, EAST, NORTH, COUNT, EASTWARD, WESTWARD, SLABS = 0, 24, 48, 56, 64, 65, 68, 71
ROWS = 32


def neighbour(north, east):
    lat, lon = lax.axis_index("lat"), lax.axis_index("lon")
    lats, lons = lax.axis_size("lat"), lax.axis_size("lon")
    return {"lat": lax.rem(lat + north + lats, lats), "lon": lax.rem(lon + east + lons, lons)}


def pack_columns(ext):
    lane = lax.broadcasted_iota(jnp.int32, (8, 128), 1)
    group = lane // HALO
    for plane in range(2):
        last = jnp.zeros((8, 128), jnp.float32)
        first = jnp.zeros((8, 128), jnp.float32)
        for slot in range(4):
            for level in range(8):
                place = 4 * level + slot
                field = ext[(4 * plane + slot) * 8 + level, 8:16, :]
                turned = pltpu.roll(field, (HALO * place + HALO) % 128, 1)
                last = jnp.where(group == place, turned, last)
                first = jnp.where(group == (place + 1) % 32, turned, first)
        ext[EASTWARD + plane, 8:16, :] = last
        ext[WESTWARD + plane, 8:16, :] = first
    turned = pltpu.roll(ext[COUNT, 8:16, :], HALO, 1)
    both = jnp.where(lane < 2 * HALO, turned, 0.0)
    for shift in (16, 32, 64):
        both = both + pltpu.roll(both, shift, 1)
    ext[EASTWARD + 2, 8:16, :] = both
    ext[WESTWARD + 2, 8:16, :] = both


def exchange_kernel(tracers, cotangent, east_vel, north_vel, sea_mask, level_count, ext, west, east, mask, count, load_sem, send_sem, recv_sem):
    around = [(a, b) for a in (-1, 0, 1) for b in (-1, 0, 1) if (a, b) != (0, 0)]
    barrier = pltpu.get_barrier_semaphore()
    for north, easterly in around:
        pl.semaphore_signal(barrier, inc=1, device_id=neighbour(north, easterly), device_id_type=MESH)
    loads = []
    for source, target in (
        (sea_mask, mask),
        (level_count, count),
        (tracers, ext.at[TRACER : TRACER + 24, 8:16, :]),
        (cotangent, ext.at[COTAN : COTAN + 24, 8:16, :]),
        (east_vel, ext.at[EAST : EAST + 8, 8:16, :]),
        (north_vel, ext.at[NORTH : NORTH + 8, 8:16, :]),
    ):
        loads.append(pltpu.make_async_copy(source, target, load_sem.at[len(loads)]))
        loads[-1].start()
    for load in loads:
        load.wait()
    ext[COUNT, 8:16, :] = jnp.where(mask[...] == 1, count[...], 0).astype(jnp.float32)
    pack_columns(ext)
    eastward, westward = slice(EASTWARD, EASTWARD + 3), slice(WESTWARD, WESTWARD + 3)
    plan = (
        (0, 1, ext.at[eastward, 8:16, :], west.at[:, 0:8, :]),
        (0, -1, ext.at[westward, 8:16, :], east.at[:, 0:8, :]),
        (1, 1, ext.at[eastward, 12:16, :], west.at[:, 12:16, :]),
        (-1, 1, ext.at[eastward, 8:12, :], west.at[:, 8:12, :]),
        (1, -1, ext.at[westward, 12:16, :], east.at[:, 12:16, :]),
        (-1, -1, ext.at[westward, 8:12, :], east.at[:, 8:12, :]),
        (1, 0, ext.at[:, 12:16, :], ext.at[:, 20:24, :]),
        (-1, 0, ext.at[:, 8:12, :], ext.at[:, 16:20, :]),
    )
    pl.semaphore_wait(barrier, len(around))
    copies = []
    for north, easterly, source, target in plan:
        copies.append(
            pltpu.make_async_remote_copy(
                src_ref=source,
                dst_ref=target,
                send_sem=send_sem.at[len(copies)],
                recv_sem=recv_sem.at[len(copies)],
                device_id=neighbour(north, easterly),
                device_id_type=MESH,
            )
        )
        copies[-1].start()
    for copy in copies:
        copy.wait_recv()
    for copy in copies:
        copy.wait_send()


def close_ring(ref, index, value):
    ref[index, 8:24, :] = value
    ref[index, 7:8, :] = value[15:16]
    ref[index, 24:25, :] = value[0:1]


def compute_kernel(ext, west, east, adj_tracers, adj_east, adj_north, strips, static, bridges, coefs, strip_coefs, states, sums, opens):
    shape = (16, 128)
    lane = lax.broadcasted_iota(jnp.int32, shape, 1)
    column = lane % 16
    level_of = (lane // 16).astype(jnp.float32)
    row = lax.broadcasted_iota(jnp.int32, shape, 0)
    lat, lats = lax.axis_index("lat"), lax.axis_size("lat")
    inside = ((row < 12) | (lat > 0)) & ((row < 8) | (row >= 12) | (lat < lats - 1))

    def turn(value, shift):
        return pltpu.roll(value, shift % 128, 1)

    def bridge(value):
        return jnp.where(column == 2, turn(value, -10), value)

    def join(quarters, slot):
        mine_last, mine_first, from_west, from_east = quarters
        joined = jnp.where(column < 4, turn(from_west, -4 * slot), turn(mine_first, -4 * slot))
        far = jnp.where(column < 12, turn(mine_last, 8 - 4 * slot), turn(from_east, 8 - 4 * slot))
        return jnp.where(column < 8, joined, far)

    for plane in range(3):
        quarters = (ext[EASTWARD + plane, 8:24, :], ext[WESTWARD + plane, 8:24, :], west[plane], east[plane])
        for slot in range(4 if plane < 2 else 1):
            field = 4 * plane + slot
            value = join(quarters, slot)
            if field < 6:
                close_ring(strips, field, value)
                bridges[field] = bridge(value)
            else:
                if field == 8:
                    value = jnp.where(inside, value, 0.0)
                close_ring(static, field - 6, value)

    counted = jnp.where(inside, ext[COUNT, 8:24, :], 0.0)
    close_ring(ext, COUNT, counted)
    ext[0:64, 7:8, :] = ext[0:64, 23:24, :]
    ext[0:64, 24:25, :] = ext[0:64, 8:9, :]

    def open_pair(is_open, velocity):
        half = velocity * 0.5
        return jnp.where(is_open, half + HORIZ, 0.0), jnp.where(is_open, half - HORIZ, 0.0)

    def stencil(wet, up, down, vel_east, vel_west, vel_north, vel_south, open_east, open_west, open_north, open_south):
        pe, qe = open_pair(open_east, vel_east)
        pw, qw = open_pair(open_west, vel_west)
        pn, qn = open_pair(open_north, vel_north)
        ps, qs = open_pair(open_south, vel_south)
        diagonal = jnp.where(wet, 1.0, 0.0) - pe + qw - pn + qs - up - down
        return diagonal, pe, pw, qe, qw, pn, ps, qn, qs, up, down

    cnt, vel_e, vel_n = static[2, 8:24, :], static[0, 8:24, :], static[1, 8:24, :]
    cnt_s, cnt_n = static[2, 7:23, :], static[2, 9:25, :]
    open_e = jnp.minimum(cnt, turn(cnt, -1))
    open_w = jnp.minimum(cnt, turn(cnt, 1))
    made = stencil(
        cnt > level_of,
        jnp.where(cnt > level_of + 1.0, VERT, 0.0),
        jnp.where((cnt > level_of) & (level_of > 0.0), VERT, 0.0),
        vel_e,
        turn(vel_e, 1),
        vel_n,
        static[1, 7:23, :],
        open_e > level_of,
        open_w > level_of,
        jnp.minimum(cnt, cnt_n) > level_of,
        jnp.minimum(cnt, cnt_s) > level_of,
    )
    for place, value in enumerate(made):
        strip_coefs[place] = value

    cnt_bridge = bridge(static[2, 8:24, :])
    cnt_bridge = turn(cnt_bridge, -3)
    vel_bridge = bridge(vel_e)
    cnt_e = jnp.where(lane == 127, cnt_bridge, turn(counted, -1))
    cnt_w = jnp.where(lane == 0, cnt_bridge, turn(counted, 1))
    least_e = jnp.minimum(counted, cnt_e)
    least_w = jnp.minimum(counted, cnt_w)
    least_n = jnp.minimum(counted, ext[COUNT, 9:25, :])
    least_s = jnp.minimum(counted, ext[COUNT, 7:23, :])

    for level in range(8):
        here = float(level)
        vel_e = ext[EAST + level, 8:24, :]
        vel_w = jnp.where(lane == 0, turn(vel_bridge, -(16 * level + 3)), turn(vel_e, 1))
        made = stencil(
            counted > here,
            jnp.where(counted > here + 1.0, VERT, 0.0),
            jnp.where(counted > here, VERT if level else 0.0, 0.0),
            vel_e,
            vel_w,
            ext[NORTH + level, 8:24, :],
            ext[NORTH + level, 7:23, :],
            least_e > here,
            least_w > here,
            least_n > here,
            least_s > here,
        )
        for place, value in enumerate(made):
            coefs[level, place] = value
        opens[0, level] = jnp.where(least_e[0:8] > here, 0.5, 0.0)
        opens[1, level] = jnp.where(least_n[0:8] > here, 0.5, 0.0)

    def strip_step(source, target, names, base):
        d, e, w, n, s, up, down = (strip_coefs[name] for name in names)
        if names is FORWARD:
            e, n = -e, -n
        else:
            w, s = -w, -s
        for tracer in range(3):
            value = source[base + tracer, 8:24, :]
            result = (
                d * value
                + e * turn(value, -1)
                + w * turn(value, 1)
                + n * source[base + tracer, 9:25, :]
                + s * source[base + tracer, 7:23, :]
                + up * turn(value, -16)
                + down * turn(value, 16)
            )
            close_ring(target, base + tracer, result)
            bridges[base + tracer] = bridge(result)

    def sides(value, base, tracer, level, rows):
        edge = pltpu.roll(bridges[base + tracer], (128 - 3) - 16 * level, 1)[:rows]
        after = jnp.where(lane[:rows] == 127, edge, turn(value, -1))
        before = jnp.where(lane[:rows] == 0, edge, turn(value, 1))
        return after, before

    def forward_step(step):
        source = ext if step == 0 else states
        origin = TRACER if step == 0 else 24 * (step - 1)
        for level in range(8):
            d, e, w, n, s, up, down = (coefs[level, name] for name in FORWARD)
            for tracer in range(3):
                slab = origin + 8 * tracer + level
                value = source[slab, 8:24, :]
                north, south = source[slab, 9:25, :], source[slab, 7:23, :]
                after, before = sides(value, 0, tracer, level, 16)
                result = d * value - e * after + w * before - n * north + s * south
                if level < 7:
                    result = result + up * source[slab + 1, 8:24, :]
                if level > 0:
                    result = result + down * source[slab - 1, 8:24, :]
                close_ring(states, 24 * step + 8 * tracer + level, result)
                sums[step, 0, 8 * tracer + level] = value[:8] + after[:8]
                sums[step, 1, 8 * tracer + level] = value[:8] + north[:8]

    def last_sums():
        for level in range(8):
            for tracer in range(3):
                slab = 48 + 8 * tracer + level
                value = states[slab, 8:16, :]
                after, before = sides(value, 0, tracer, level, 8)
                sums[3, 0, 8 * tracer + level] = value + after
                sums[3, 1, 8 * tracer + level] = value + states[slab, 9:17, :]

    for step in range(3):
        forward_step(step)
        strip_step(strips, strips, FORWARD, 0)
    last_sums()

    def adjoint_step(step):
        source = ext if step == 0 else states
        origin = COTAN if step == 0 else 24 * (step - 1)
        rows = 16 if step < 3 else 8
        for level in range(8):
            d, e, w, n, s, up, down = (coefs[level, name, :rows] for name in ADJOINT)
            grad_e = jnp.zeros((8, 128), jnp.float32)
            grad_n = jnp.zeros((8, 128), jnp.float32)
            for tracer in range(3):
                slab = origin + 8 * tracer + level
                value = source[slab, 8 : 8 + rows, :]
                north, south = source[slab, 9 : 9 + rows, :], source[slab, 7 : 7 + rows, :]
                after, before = sides(value, 3, tracer, level, rows)
                result = d * value + e * after - w * before + n * north - s * south
                if level < 7:
                    result = result + up * source[slab + 1, 8 : 8 + rows, :]
                if level > 0:
                    result = result + down * source[slab - 1, 8 : 8 + rows, :]
                if step < 3:
                    close_ring(states, 24 * step + 8 * tracer + level, result)
                else:
                    adj_tracers[8 * tracer + level] = result
                grad_e = grad_e + sums[3 - step, 0, 8 * tracer + level] * (after[:8] - value[:8])
                grad_n = grad_n + sums[3 - step, 1, 8 * tracer + level] * (north[:8] - value[:8])
            if step > 0:
                grad_e = grad_e + adj_east[level]
                grad_n = grad_n + adj_north[level]
            if step == 3:
                grad_e = grad_e * opens[0, level]
                grad_n = grad_n * opens[1, level]
            adj_east[level] = grad_e
            adj_north[level] = grad_n

    for step in range(4):
        adjoint_step(step)
        if step < 3:
            strip_step(strips, strips, ADJOINT, 3)


FORWARD = (0, 3, 2, 7, 6, 9, 10)
ADJOINT = (0, 1, 4, 5, 8, 9, 10)


def on_device(tracers, cotangent, east_vel, north_vel, sea_mask, level_count):
    f32 = jnp.float32
    hbm = pl.BlockSpec(memory_space=pltpu.HBM)
    anywhere = pl.BlockSpec(memory_space=pl.ANY)
    vmem = pl.BlockSpec(memory_space=pltpu.VMEM)
    exchanged = pl.pallas_call(
        exchange_kernel,
        name="exchange",
        out_shape=(
            jax.ShapeDtypeStruct((SLABS, ROWS, 128), f32),
            jax.ShapeDtypeStruct((3, 16, 128), f32),
            jax.ShapeDtypeStruct((3, 16, 128), f32),
        ),
        in_specs=[hbm] * 6,
        out_specs=(vmem,) * 3,
        scratch_shapes=[
            pltpu.VMEM((8, 128), jnp.int32),
            pltpu.VMEM((8, 128), jnp.int32),
            pltpu.SemaphoreType.DMA((6,)),
            pltpu.SemaphoreType.DMA((8,)),
            pltpu.SemaphoreType.DMA((8,)),
        ],
        compiler_params=pltpu.CompilerParams(collective_id=0, has_side_effects=True, vmem_limit_bytes=8 << 20),
    )(*(pltpu.with_memory_space_constraint(x, pltpu.HBM) for x in (tracers.reshape(24, 8, 128), cotangent.reshape(24, 8, 128), east_vel, north_vel, sea_mask, level_count)))
    adj_tracers, adj_east, adj_north = pl.pallas_call(
        compute_kernel,
        name="compute",
        out_shape=(
            jax.ShapeDtypeStruct((24, 8, 128), f32),
            jax.ShapeDtypeStruct((8, 8, 128), f32),
            jax.ShapeDtypeStruct((8, 8, 128), f32),
        ),
        in_specs=[vmem] * 3,
        out_specs=(vmem,) * 3,
        scratch_shapes=[
            pltpu.VMEM((6, ROWS, 128), f32),
            pltpu.VMEM((3, ROWS, 128), f32),
            pltpu.VMEM((6, 16, 128), f32),
            pltpu.VMEM((8, 11, 16, 128), f32),
            pltpu.VMEM((11, 16, 128), f32),
            pltpu.VMEM((72, ROWS, 128), f32),
            pltpu.VMEM((4, 2, 24, 8, 128), f32),
            pltpu.VMEM((2, 8, 8, 128), f32),
        ],
        compiler_params=pltpu.CompilerParams(vmem_limit_bytes=16 << 20),
    )(*exchanged)
    return adj_tracers.reshape(tracers.shape), adj_east, adj_north


def solution(mesh):
    placed = (
        P(None, None, "lat", "lon"),
        P(None, None, "lat", "lon"),
        P(None, "lat", "lon"),
        P(None, "lat", "lon"),
        P("lat", "lon"),
        P("lat", "lon"),
    )
    return jax.shard_map(
        on_device,
        mesh=mesh,
        in_specs=placed,
        out_specs=(P(None, None, "lat", "lon"), P(None, "lat", "lon"), P(None, "lat", "lon")),
        check_vma=False,
    )
```

```python
import jax
import jax.numpy as jnp
from jax import lax
from jax.experimental import pallas as pl
from jax.experimental.pallas import tpu as pltpu
from jax.sharding import PartitionSpec as P

MESH = pl.DeviceIdType.MESH
HALO = 4
HORIZ = 0.22
VERT = 0.05
LEVELS = 8
TRACERS = 3
UNROLL = 2

TRACER, COTAN, EAST, NORTH, COUNT, PLANES = 0, 24, 48, 56, 64, 65
ROWS = 32
STRIPS = 17
FORWARD = (0, 3, 2, 7, 6, 9, 10)
ADJOINT = (0, 1, 4, 5, 8, 9, 10)


def turn(value, shift):
    return pltpu.roll(value, shift % 128, 1)


def lanes_of(rows):
    return lax.broadcasted_iota(jnp.int32, (rows, 128), 1)


def inside_grid():
    row = lax.broadcasted_iota(jnp.int32, (16, 128), 0)
    lat, lats = lax.axis_index("lat"), lax.axis_size("lat")
    return ((row < 12) | (lat > 0)) & ((row < 8) | (row >= 12) | (lat < lats - 1))


def close_ring(ref, index, value):
    ref[index, 8:24, :] = value
    ref[index, 7:8, :] = value[15:16]
    ref[index, 24:25, :] = value[0:1]


def open_pair(is_open, velocity):
    half = velocity * 0.5
    return jnp.where(is_open, half + HORIZ, 0.0), jnp.where(is_open, half - HORIZ, 0.0)


def stencil(wet, up, down, vel_east, vel_west, vel_north, vel_south, open_east, open_west, open_north, open_south):
    pe, qe = open_pair(open_east, vel_east)
    pw, qw = open_pair(open_west, vel_west)
    pn, qn = open_pair(open_north, vel_north)
    ps, qs = open_pair(open_south, vel_south)
    diagonal = jnp.where(wet, 1.0, 0.0) - pe + qw - pn + qs - up - down
    return diagonal, pe, pw, qe, qw, pn, ps, qn, qs, up, down


def neighbour(north, east):
    lat, lon = lax.axis_index("lat"), lax.axis_index("lon")
    lats, lons = lax.axis_size("lat"), lax.axis_size("lon")
    return {"lat": lax.rem(lat + north + lats, lats), "lon": lax.rem(lon + east + lons, lons)}


def greetings(side):
    place, places = lax.axis_index("lon"), lax.axis_size("lon")
    if places < 3:
        return place >= 0, place >= 0
    if side > 0:
        return (place != places - 1) & (place != places - 2), place >= 0
    return place >= 0, (place != places - 1) & (place != 0)


def pack_ends(ext, packed):
    group = lanes_of(8) // HALO
    for half in range(2):
        last = jnp.zeros((8, 128), jnp.float32)
        first = jnp.zeros((8, 128), jnp.float32)
        for field in range(8):
            for i in range(4):
                place = 8 * i + field
                turned = turn(ext[8 * field + 2 * i + half, 8:16, :], HALO * (place + 1))
                last = jnp.where(group == place, turned, last)
                first = jnp.where(group == (place + 1) % 32, turned, first)
        packed[half] = last
        packed[3 + half] = first
    both = jnp.where(group < 2, turn(ext[COUNT, 8:16, :], HALO), 0.0)
    for shift in (32, 64):
        both = both + turn(both, shift)
    packed[2] = both
    packed[5] = both


def pack_strips(ext, own):
    lane = lanes_of(16)
    group, place = lane // 32, lane % 32

    def spread(value):
        return jnp.where(place < 12, turn(value, -12), turn(value, 4))

    for field in range(8):
        for half in range(2):
            gathered = jnp.zeros((16, 128), jnp.float32)
            for i in range(4):
                turned = turn(ext[8 * field + 2 * i + half, 8:24, :], 32 * i + 16)
                gathered = jnp.where(group == i, turned, gathered)
            own[2 * field + half] = spread(gathered)
    gathered = jnp.where(lane < 32, turn(ext[COUNT, 8:24, :], 16), 0.0)
    for shift in (32, 64):
        gathered = gathered + turn(gathered, shift)
    own[16] = spread(gathered)


def exchange_kernel(
    tracers, cotangent, east_vel, north_vel, sea_mask, level_count,
    adj_tracers, adj_east, adj_north, own, west, east,
    ext, packed, mask, count, coefs, opens, states, sums, load_sem, send_sem, recv_sem, answer_sem,
):
    loads = []
    for source, target in (
        (tracers, ext.at[TRACER : TRACER + 24, 8:16, :]),
        (cotangent, ext.at[COTAN : COTAN + 24, 8:16, :]),
        (east_vel, ext.at[EAST : EAST + 8, 8:16, :]),
        (north_vel, ext.at[NORTH : NORTH + 8, 8:16, :]),
        (sea_mask, mask),
        (level_count, count),
    ):
        loads.append(pltpu.make_async_copy(source, target, load_sem.at[len(loads)]))
        loads[-1].start()

    lat, lats, lon, lons = lax.axis_index("lat"), lax.axis_size("lat"), lax.axis_index("lon"), lax.axis_size("lon")
    exists = {0: lat >= 0, 1: lat < lats - 1, -1: lat > 0}
    barrier = pltpu.get_barrier_semaphore()
    in_column = jnp.where(exists[1], 1, 0) + jnp.where(exists[-1], 1, 0)
    expected = in_column
    for side in (-1, 1):
        greets, greeted = greetings(side)
        expected = expected + jnp.where(greeted, in_column + 1, 0)
        for north in (0, 1, -1):

            @pl.when(greets & exists[north])
            def _():
                pl.semaphore_signal(barrier, inc=1, device_id=neighbour(north, side), device_id_type=MESH)

    for north in (1, -1):

        @pl.when(exists[north])
        def _():
            pl.semaphore_signal(barrier, inc=1, device_id=neighbour(north, 0), device_id_type=MESH)

    for north, rows in ((1, slice(8, 12)), (-1, slice(12, 16))):

        @pl.when(~exists[north])
        def _():
            west[:, rows, :] = jnp.zeros((3, 4, 128), jnp.float32)
            east[:, rows, :] = jnp.zeros((3, 4, 128), jnp.float32)
            ext[:, rows.start + 8 : rows.stop + 8, :] = jnp.zeros((PLANES, 4, 128), jnp.float32)

    plan = (
        (0, 1, packed.at[0:3], west.at[:, 0:8, :]),
        (1, 1, packed.at[0:3, 4:8, :], west.at[:, 12:16, :]),
        (-1, 1, packed.at[0:3, 0:4, :], west.at[:, 8:12, :]),
        (0, -1, packed.at[3:6], east.at[:, 0:8, :]),
        (1, -1, packed.at[3:6, 4:8, :], east.at[:, 12:16, :]),
        (-1, -1, packed.at[3:6, 0:4, :], east.at[:, 8:12, :]),
        (1, 0, ext.at[:, 12:16, :], ext.at[:, 20:24, :]),
        (-1, 0, ext.at[:, 8:12, :], ext.at[:, 16:20, :]),
    )
    copies = []
    for north, easterly, source, target in plan:
        copy = pltpu.make_async_remote_copy(
            src_ref=source,
            dst_ref=target,
            send_sem=send_sem.at[len(copies)],
            recv_sem=recv_sem.at[len(copies)],
            device_id=neighbour(north, easterly),
            device_id_type=MESH,
        )
        copies.append((copy, exists[north], exists[-north]))

    def start(chosen, condition):
        for copy, sent, _ in chosen:
            pl.when(sent & condition)(copy.start)

    def wait_recv(chosen):
        for copy, _, received in chosen:
            pl.when(received)(copy.wait_recv)

    def answer(side, theirs):
        for north in (0, 1, -1):

            @pl.when(~greetings(side)[0] & exists[north])
            def _():
                pl.semaphore_signal(theirs, inc=1, device_id=neighbour(north, side), device_id_type=MESH)

    eastward, westward, along = copies[0:3], copies[3:6], copies[6:8]
    first, last = lon == 0, lon == lons - 1
    pl.semaphore_wait(barrier, expected)
    answer(1, answer_sem.at[0])
    for load in loads:
        load.wait()
    ext[COUNT, 8:16, :] = jnp.where(mask[...] == 1, count[...], 0).astype(jnp.float32)
    pack_ends(ext, packed)
    start(eastward, lon >= 0)
    greeted = greetings(-1)[1]
    start(westward, greeted)
    start(along, lon >= 0)

    def start_answered(condition):
        @pl.when(condition)
        def _():
            pl.semaphore_wait(answer_sem.at[0], in_column + 1)

        start(westward, condition)

    start_answered(~greeted & last)
    wait_recv(along)
    interior(ext, adj_tracers, adj_east, adj_north, coefs, opens, states, sums)
    pack_strips(ext, own)
    start_answered(~greeted & first)
    wait_recv(eastward)
    wait_recv(westward)
    for copy, sent, _ in copies:
        pl.when(sent)(copy.wait_send)


def interior(ext, adj_tracers, adj_east, adj_north, coefs, opens, states, sums):
    margins = jnp.where(inside_grid()[8:16], ext[COUNT, 16:24, :], 0.0)
    ext[COUNT, 16:24, :] = margins
    ext[COUNT, 7:8, :] = margins[7:8]
    ext[COUNT, 24:25, :] = ext[COUNT, 8:9, :]

    def each_level(body):
        def step(level, carry):
            body(level)
            return carry

        lax.fori_loop(0, LEVELS, step, 0, unroll=UNROLL)

    def repeat_ends(level):
        for field in range(8):
            ext[8 * field + level, 7:8, :] = ext[8 * field + level, 23:24, :]
            ext[8 * field + level, 24:25, :] = ext[8 * field + level, 8:9, :]

    each_level(repeat_ends)

    def coefficients(level):
        here = level.astype(jnp.float32)
        cnt = ext[COUNT, 8:24, :]
        vel_e = ext[EAST + level, 8:24, :]
        open_e = jnp.minimum(cnt, turn(cnt, -1)) > here
        open_n = jnp.minimum(cnt, ext[COUNT, 9:25, :]) > here
        made = stencil(
            cnt > here,
            jnp.where(cnt > here + 1.0, VERT, 0.0),
            jnp.where(cnt > here, jnp.where(level > 0, VERT, 0.0), 0.0),
            vel_e,
            turn(vel_e, 1),
            ext[NORTH + level, 8:24, :],
            ext[NORTH + level, 7:23, :],
            open_e,
            jnp.minimum(cnt, turn(cnt, 1)) > here,
            open_n,
            jnp.minimum(cnt, ext[COUNT, 7:23, :]) > here,
        )
        for place, value in enumerate(made):
            coefs[level, place] = value
        opens[level, 0] = jnp.where(open_e[0:8], 0.5, 0.0)
        opens[level, 1] = jnp.where(open_n[0:8], 0.5, 0.0)

    each_level(coefficients)

    def near(source, origin, tracer, level, rows):
        base = origin + LEVELS * tracer
        value = source[base + level, 8 : 8 + rows, :]
        north, south = source[base + level, 9 : 9 + rows, :], source[base + level, 7 : 7 + rows, :]
        above = source[base + jnp.minimum(level + 1, LEVELS - 1), 8 : 8 + rows, :]
        below = source[base + jnp.maximum(level - 1, 0), 8 : 8 + rows, :]
        return value, turn(value, -1), turn(value, 1), north, south, above, below

    def forward_step(step, level):
        source = ext if step == 0 else states
        origin = TRACER if step == 0 else 24 * (step - 1)
        d, e, w, n, s, up, down = (coefs[level, name] for name in FORWARD)
        for tracer in range(TRACERS):
            value, after, before, north, south, above, below = near(source, origin, tracer, level, 16)
            result = d * value - e * after + w * before - n * north + s * south + up * above + down * below
            close_ring(states, 24 * step + LEVELS * tracer + level, result)
            sums[step, 0, LEVELS * tracer + level] = value[:8] + after[:8]
            sums[step, 1, LEVELS * tracer + level] = value[:8] + north[:8]

    def last_sums(level):
        for tracer in range(TRACERS):
            slab = 48 + LEVELS * tracer + level
            value = states[slab, 8:16, :]
            sums[3, 0, LEVELS * tracer + level] = value + turn(value, -1)
            sums[3, 1, LEVELS * tracer + level] = value + states[slab, 9:17, :]

    def adjoint_step(step, level):
        source = ext if step == 0 else states
        origin = COTAN if step == 0 else 24 * (step - 1)
        rows = 16 if step < 3 else 8
        d, e, w, n, s, up, down = (coefs[level, name, :rows] for name in ADJOINT)
        grad_e = jnp.zeros((8, 128), jnp.float32)
        grad_n = jnp.zeros((8, 128), jnp.float32)
        for tracer in range(TRACERS):
            value, after, before, north, south, above, below = near(source, origin, tracer, level, rows)
            result = d * value + e * after - w * before + n * north - s * south + up * above + down * below
            if step < 3:
                close_ring(states, 24 * step + LEVELS * tracer + level, result)
            else:
                adj_tracers[LEVELS * tracer + level] = result
            grad_e = grad_e + sums[3 - step, 0, LEVELS * tracer + level] * (after[:8] - value[:8])
            grad_n = grad_n + sums[3 - step, 1, LEVELS * tracer + level] * (north[:8] - value[:8])
        if step > 0:
            grad_e = grad_e + adj_east[level]
            grad_n = grad_n + adj_north[level]
        if step == 3:
            grad_e = grad_e * opens[level, 0]
            grad_n = grad_n * opens[level, 1]
        adj_east[level] = grad_e
        adj_north[level] = grad_n

    for step in range(3):
        each_level(lambda level, step=step: forward_step(step, level))
    each_level(last_sums)
    for step in range(4):
        each_level(lambda level, step=step: adjoint_step(step, level))


def ends_kernel(part_tracers, part_east, part_north, own, west, east, adj_tracers, adj_east, adj_north, rings):
    lane = lanes_of(16)
    place = lane % 32
    inside = inside_grid()

    def joined(field, half):
        index = 2 * field + half
        source = half if field < 8 else 2
        shift = 4 * field if field < 8 else 0
        value = jnp.where(place < 4, turn(west[source], -shift), own[index])
        return jnp.where((place >= 20) & (place < 24), turn(east[source], 16 - shift), value)

    def stored(field, half, value):
        close_ring(rings, 2 * field + half, value)
        return value

    count = stored(8, 0, jnp.where(inside, joined(8, 0), 0.0))
    counts = (count, turn(count, -1), turn(count, 1), rings[16, 9:25, :], rings[16, 7:23, :])
    least = [jnp.minimum(count, other) for other in counts]
    made, opens = [], []
    for half in range(2):
        level = (2 * (lane // 32) + half).astype(jnp.float32)
        vel_e = joined(6, half)
        vel_n = stored(7, half, joined(7, half))
        opened = [value > level for value in least]
        made.append(
            stencil(
                opened[0],
                jnp.where(count > level + 1.0, VERT, 0.0),
                jnp.where(opened[0] & (level > 0.0), VERT, 0.0),
                vel_e,
                turn(vel_e, 1),
                vel_n,
                rings[14 + half, 7:23, :],
                *opened[1:],
            )
        )
        opens.append([jnp.where(opened[which][:8], 0.5, 0.0) for which in (1, 3)])

    def advanced(field, values, names, rows):
        near = []
        for half in range(2):
            value = values[half]
            ring = 2 * field + half
            near.append((value, turn(value, -1), turn(value, 1), rings[ring, 9 : 9 + rows, :], rings[ring, 7 : 7 + rows, :]))
        results = []
        for half in range(2):
            value, after, before, north, south = near[half]
            d, e, w, n, s, up, down = (made[half][name][:rows] for name in names)
            above = values[1] if half == 0 else turn(values[0], -32)
            below = turn(values[1], 32) if half == 0 else values[0]
            if names is FORWARD:
                result = d * value - e * after + w * before - n * north + s * south
            else:
                result = d * value + e * after - w * before + n * north - s * south
            results.append(result + up * above + down * below)
        return results, near

    fields = [[stored(field, half, joined(field, half)) for half in range(2)] for field in range(6)]
    sums = []
    for step in range(4):
        sums.append([])
        for tracer in range(TRACERS):
            if step < 3:
                results, near = advanced(tracer, fields[tracer], FORWARD, 16)
            else:
                results = fields[tracer]
                near = [(value, turn(value, -1), None, rings[2 * tracer + half, 9:25, :]) for half, value in enumerate(results)]
            sums[step].append([(value[:8] + after[:8], value[:8] + north[:8]) for value, after, _, north, *_ in near])
            if step < 3:
                fields[tracer] = [stored(tracer, half, value) for half, value in enumerate(results)]
    grads = [[jnp.zeros((8, 128), jnp.float32)] * 2 for half in range(2)]
    for step in range(4):
        for tracer in range(TRACERS):
            rows = 16 if step < 3 else 8
            values = [value[:rows] for value in fields[3 + tracer]]
            results, near = advanced(3 + tracer, values, ADJOINT, rows)
            for half in range(2):
                value, after, _, north, _ = near[half]
                east_sum, north_sum = sums[3 - step][tracer][half]
                grads[half] = [
                    grads[half][0] + east_sum * (after[:8] - value[:8]),
                    grads[half][1] + north_sum * (north[:8] - value[:8]),
                ]
            fields[3 + tracer] = [stored(3 + tracer, half, value) if step < 3 else value for half, value in enumerate(results)]

    short = lanes_of(8)
    at_end = (short < 4) | (short >= 124)
    short_place = short % 32

    def patched(value, part, target, half, base):
        value = jnp.where(short_place < 4, turn(value, -16), value)
        for i in range(4):
            slab = base + 2 * i + half
            target[slab] = jnp.where(at_end, turn(value, -(32 * i + 4)), part[slab])

    for half in range(2):
        for tracer in range(TRACERS):
            patched(fields[3 + tracer][half], part_tracers, adj_tracers, half, LEVELS * tracer)
        patched(grads[half][0] * opens[half][0], part_east, adj_east, half, 0)
        patched(grads[half][1] * opens[half][1], part_north, adj_north, half, 0)


def on_device(tracers, cotangent, east_vel, north_vel, sea_mask, level_count):
    f32 = jnp.float32
    vmem = pl.BlockSpec(memory_space=pltpu.VMEM)
    operands = (tracers.reshape(24, 8, 128), cotangent.reshape(24, 8, 128), east_vel, north_vel, sea_mask, level_count)
    results = (
        jax.ShapeDtypeStruct((24, 8, 128), f32),
        jax.ShapeDtypeStruct((8, 8, 128), f32),
        jax.ShapeDtypeStruct((8, 8, 128), f32),
    )
    parts = pl.pallas_call(
        exchange_kernel,
        name="exchange",
        out_shape=(
            *results,
            jax.ShapeDtypeStruct((STRIPS, 16, 128), f32),
            jax.ShapeDtypeStruct((3, 16, 128), f32),
            jax.ShapeDtypeStruct((3, 16, 128), f32),
        ),
        in_specs=[pl.BlockSpec(memory_space=pltpu.HBM)] * 6,
        out_specs=(vmem,) * 6,
        scratch_shapes=[
            pltpu.VMEM((PLANES, ROWS, 128), f32),
            pltpu.VMEM((6, 8, 128), f32),
            pltpu.VMEM((8, 128), jnp.int32),
            pltpu.VMEM((8, 128), jnp.int32),
            pltpu.VMEM((LEVELS, 11, 16, 128), f32),
            pltpu.VMEM((LEVELS, 2, 8, 128), f32),
            pltpu.VMEM((72, ROWS, 128), f32),
            pltpu.VMEM((4, 2, 24, 8, 128), f32),
            pltpu.SemaphoreType.DMA((6,)),
            pltpu.SemaphoreType.DMA((8,)),
            pltpu.SemaphoreType.DMA((8,)),
            pltpu.SemaphoreType.REGULAR((1,)),
        ],
        compiler_params=pltpu.CompilerParams(collective_id=0, has_side_effects=True, vmem_limit_bytes=16 << 20),
    )(*(pltpu.with_memory_space_constraint(operand, pltpu.HBM) for operand in operands))
    adj_tracers, adj_east, adj_north = pl.pallas_call(
        ends_kernel,
        name="ends",
        out_shape=results,
        in_specs=[vmem] * 6,
        out_specs=(vmem,) * 3,
        scratch_shapes=[pltpu.VMEM((STRIPS, ROWS, 128), f32)],
        compiler_params=pltpu.CompilerParams(vmem_limit_bytes=16 << 20),
    )(*parts)
    return adj_tracers.reshape(tracers.shape), adj_east, adj_north


def solution(mesh):
    placed = (
        P(None, None, "lat", "lon"),
        P(None, None, "lat", "lon"),
        P(None, "lat", "lon"),
        P(None, "lat", "lon"),
        P("lat", "lon"),
        P("lat", "lon"),
    )
    return jax.shard_map(
        on_device,
        mesh=mesh,
        in_specs=placed,
        out_specs=(P(None, None, "lat", "lon"), P(None, "lat", "lon"), P(None, "lat", "lon")),
        check_vma=False,
    )
```

```python
import jax
import jax.numpy as jnp
from jax import lax
from jax.experimental import pallas as pl
from jax.experimental.pallas import tpu as pltpu
from jax.sharding import PartitionSpec as P

MESH = pl.DeviceIdType.MESH
HALO = 4
HORIZ = 0.22
VERT = 0.05
LEVELS = 8
TRACERS = 3
UNROLL = 2

TRACER, COTAN, EAST, NORTH, COUNT, PLANES = 0, 24, 48, 56, 64, 65
ROWS = 32
STRIPS = 9
SPARE = (0, 1, 2, 7)
FORWARD = (0, 3, 2, 7, 6, 9, 10)
ADJOINT = (0, 1, 4, 5, 8, 9, 10)


def turn(value, shift):
    return pltpu.roll(value, shift % 128, 1)


def lanes_of(rows):
    return lax.broadcasted_iota(jnp.int32, (rows, 128), 1)


def close_ring(ref, index, value):
    ref[index, 8:24, :] = value
    ref[index, 7:8, :] = value[15:16]
    ref[index, 24:25, :] = value[0:1]


def open_pair(is_open, velocity):
    half = velocity * 0.5
    return jnp.where(is_open, half + HORIZ, 0.0), jnp.where(is_open, half - HORIZ, 0.0)


def stencil(wet, up, down, vel_east, vel_west, vel_north, vel_south, open_east, open_west, open_north, open_south):
    pe, qe = open_pair(open_east, vel_east)
    pw, qw = open_pair(open_west, vel_west)
    pn, qn = open_pair(open_north, vel_north)
    ps, qs = open_pair(open_south, vel_south)
    diagonal = jnp.where(wet, 1.0, 0.0) - pe + qw - pn + qs - up - down
    return diagonal, pe, pw, qe, qw, pn, ps, qn, qs, up, down


def neighbours():
    lat, lon = lax.axis_index("lat"), lax.axis_index("lon")
    last_lat, last_lon = lax.axis_size("lat") - 1, lax.axis_size("lon") - 1
    lats = {0: lat, 1: jnp.where(lat == last_lat, 0, lat + 1), -1: jnp.where(lat == 0, last_lat, lat - 1)}
    lons = {0: lon, 1: jnp.where(lon == last_lon, 0, lon + 1), -1: jnp.where(lon == 0, last_lon, lon - 1)}
    return lambda north, east: {"lat": lats[north], "lon": lons[east]}


def greetings(side):
    place, places = lax.axis_index("lon"), lax.axis_size("lon")
    if places < 3:
        return place >= 0, place >= 0
    if side > 0:
        return (place != places - 1) & (place != places - 2), place >= 0
    return place >= 0, (place != places - 1) & (place != 0)


def pack_ends(ext, packed):
    lane = lanes_of(8)
    group = lane // HALO
    counts = ext[COUNT, 8:16, :]
    spread = jnp.zeros((8, 128), jnp.float32)
    for column, field in enumerate(SPARE):
        spread = jnp.where(lane == HALO * field, turn(counts, HALO * field - 124 - column), spread)
    for shift in (32, 64):
        spread = spread + turn(spread, shift)
    is_spare = (lane % 32 == 0) | (lane % 32 == 4) | (lane % 32 == 8) | (lane % 32 == 28)
    for half in range(2):
        last = jnp.zeros((8, 128), jnp.float32)
        first = jnp.zeros((8, 128), jnp.float32)
        for field in range(8):
            for i in range(4):
                place = 8 * i + field
                turned = turn(ext[8 * field + 2 * i + half, 8:16, :], HALO * (place + 1))
                last = jnp.where(group == place, turned, last)
                first = jnp.where(group == (place + 1) % 32, turned, first)
        if half == 0:
            for i in range(4):
                first = jnp.where(lane == (32 * i + 35) % 128, turn(counts, 31 * i + 35), first)
        packed[half] = jnp.where(is_spare, spread, last)
        packed[2 + half] = first


def pack_strips(ext, own):
    lane = lanes_of(16)
    for field in range(8):
        gathered = jnp.zeros((16, 128), jnp.float32)
        for level in range(LEVELS):
            gathered = jnp.where(lane // 16 == level, turn(ext[8 * field + level, 8:24, :], 16 * level + 8), gathered)
        own[field] = gathered
    gathered = jnp.where(lane < 16, turn(ext[COUNT, 8:24, :], 8), 0.0)
    for shift in (16, 32, 64):
        gathered = gathered + turn(gathered, shift)
    own[8] = gathered


def run_strip(fields, count):
    level = (lanes_of(16) // 16).astype(jnp.float32)

    def north_of(value):
        return pltpu.roll(value, 15, 0)

    def south_of(value):
        return pltpu.roll(value, 1, 0)

    vel_e, vel_n = fields[6], fields[7]
    counts = (count, turn(count, -1), turn(count, 1), north_of(count), south_of(count))
    opened = [jnp.minimum(count, other) > level for other in counts]
    made = stencil(
        opened[0],
        jnp.where(count > level + 1.0, VERT, 0.0),
        jnp.where(opened[0] & (level > 0.0), VERT, 0.0),
        vel_e,
        turn(vel_e, 1),
        vel_n,
        south_of(vel_n),
        *opened[1:],
    )
    opens = [jnp.where(opened[which][:8], 0.5, 0.0) for which in (1, 3)]

    def advanced(value, after, before, north, south, names, rows):
        above, below = turn(value, -16), turn(value, 16)
        d, e, w, n, s, up, down = (made[name][:rows] for name in names)
        value, after, before, north, south, above, below = (item[:rows] for item in (value, after, before, north, south, above, below))
        if names is FORWARD:
            return (d * value - e * after) + (w * before - n * north) + (s * south + (up * above + down * below))
        return (d * value + e * after) + (n * north - w * before) + ((up * above + down * below) - s * south)

    fields = list(fields[:6])
    sums, slopes = {}, {}
    for step in range(4):
        for tracer in range(TRACERS):
            value = fields[tracer]
            after, north = turn(value, -1), north_of(value)
            sums[step, tracer] = ((value + after)[:8], (value + north)[:8])
            if step < 3:
                fields[tracer] = advanced(value, after, turn(value, 1), north, south_of(value), FORWARD, 16)
            value = fields[3 + tracer]
            after, north = turn(value, -1), north_of(value)
            slopes[step, tracer] = ((after - value)[:8], (north - value)[:8])
            fields[3 + tracer] = advanced(value, after, turn(value, 1), north, south_of(value), ADJOINT, 16 if step < 3 else 8)
    grads = []
    for which in range(2):
        total = None
        for step in (1, 2, 0, 3):
            for tracer in range(TRACERS):
                term = sums[step, tracer][which] * slopes[3 - step, tracer][which]
                total = term if total is None else total + term
        grads.append(total * opens[which])
    return fields[3:], grads


def patch(strip, parts, targets, shift, at_end):
    states, grads = strip
    for part, target, base, value in (
        *((parts[0], targets[0], LEVELS * tracer, value) for tracer, value in enumerate(states)),
        (parts[1], targets[1], 0, grads[0]),
        (parts[2], targets[2], 0, grads[1]),
    ):
        for level in range(LEVELS):
            target[base + level] = jnp.where(at_end, turn(value, shift - 16 * level), part[base + level])


def eastern_strip(own, east, adj_tracers, adj_east, adj_north):
    lane = lanes_of(16)
    place = lane % 16
    outer = (place >= 8) & (place < 12)
    odd = lane % 32 >= 16
    fields = []
    for field in range(8):
        arrived = jnp.where(odd, turn(east[1], 20 - 4 * field), turn(east[0], 4 - 4 * field))
        fields.append(jnp.where(outer, arrived, own[field]))
    spread = jnp.zeros((16, 128), jnp.float32)
    for i in range(4):
        spread = jnp.where(lane == 8 + i, turn(east[0], -27 - 31 * i), spread)
    for shift in (16, 32, 64):
        spread = spread + turn(spread, shift)
    parts = (adj_tracers, adj_east, adj_north)
    patch(run_strip(fields, jnp.where(outer, spread, own[8])), parts, parts, 120, lanes_of(8) >= 124)


def exchange_kernel(
    tracers, cotangent, east_vel, north_vel, sea_mask, level_count,
    adj_tracers, adj_east, adj_north, own_west, west,
    ext, own, east, packed, mask, count, coefs, opens, states, sums, load_sem, send_sem, recv_sem, answer_sem,
):
    loads = []
    for source, target in (
        (tracers, ext.at[TRACER : TRACER + 24, 8:16, :]),
        (cotangent, ext.at[COTAN : COTAN + 24, 8:16, :]),
        (east_vel, ext.at[EAST : EAST + 8, 8:16, :]),
        (north_vel, ext.at[NORTH : NORTH + 8, 8:16, :]),
        (sea_mask, mask),
        (level_count, count),
    ):
        loads.append(pltpu.make_async_copy(source, target, load_sem.at[len(loads)]))
        loads[-1].start()

    neighbour = neighbours()
    lat, lats, lon, lons = lax.axis_index("lat"), lax.axis_size("lat"), lax.axis_index("lon"), lax.axis_size("lon")
    exists = {0: lat >= 0, 1: lat < lats - 1, -1: lat > 0}
    barrier = pltpu.get_barrier_semaphore()
    in_column = jnp.where(exists[1], 1, 0) + jnp.where(exists[-1], 1, 0)
    expected = in_column
    for side in (-1, 1):
        greets, greeted = greetings(side)
        expected = expected + jnp.where(greeted, in_column + 1, 0)
        for north in (0, 1, -1):

            @pl.when(greets & exists[north])
            def _():
                pl.semaphore_signal(barrier, inc=1, device_id=neighbour(north, side), device_id_type=MESH)

    for north in (1, -1):

        @pl.when(exists[north])
        def _():
            pl.semaphore_signal(barrier, inc=1, device_id=neighbour(north, 0), device_id_type=MESH)

    for north, rows in ((1, slice(8, 12)), (-1, slice(12, 16))):

        @pl.when(~exists[north])
        def _():
            west[:, rows, :] = jnp.zeros((2, 4, 128), jnp.float32)
            east[:, rows, :] = jnp.zeros((2, 4, 128), jnp.float32)
            ext[:, rows.start + 8 : rows.stop + 8, :] = jnp.zeros((PLANES, 4, 128), jnp.float32)

    west[:, 11:13, :] = jnp.zeros((2, 2, 128), jnp.float32)
    east[:, 11:13, :] = jnp.zeros((2, 2, 128), jnp.float32)
    plan = (
        (0, 1, packed.at[0:2], west.at[:, 0:8, :]),
        (1, 1, packed.at[0:2, 5:8, :], west.at[:, 13:16, :]),
        (-1, 1, packed.at[0:2, 0:3, :], west.at[:, 8:11, :]),
        (0, -1, packed.at[2:4], east.at[:, 0:8, :]),
        (1, -1, packed.at[2:4, 5:8, :], east.at[:, 13:16, :]),
        (-1, -1, packed.at[2:4, 0:3, :], east.at[:, 8:11, :]),
        (1, 0, ext.at[:, 12:16, :], ext.at[:, 20:24, :]),
        (-1, 0, ext.at[:, 8:12, :], ext.at[:, 16:20, :]),
    )
    copies = []
    for north, easterly, source, target in plan:
        copy = pltpu.make_async_remote_copy(
            src_ref=source,
            dst_ref=target,
            send_sem=send_sem.at[len(copies)],
            recv_sem=recv_sem.at[len(copies)],
            device_id=neighbour(north, easterly),
            device_id_type=MESH,
        )
        copies.append((copy, exists[north], exists[-north]))

    def start(chosen, condition):
        for copy, sent, _ in chosen:
            pl.when(sent & condition)(copy.start)

    def wait_recv(chosen):
        for copy, _, received in chosen:
            pl.when(received)(copy.wait_recv)

    def answer(side, theirs):
        for north in (0, 1, -1):

            @pl.when(~greetings(side)[0] & exists[north])
            def _():
                pl.semaphore_signal(theirs, inc=1, device_id=neighbour(north, side), device_id_type=MESH)

    eastward, westward, along = copies[0:3], copies[3:6], copies[6:8]
    first, last = lon == 0, lon == lons - 1
    pl.semaphore_wait(barrier, expected)
    answer(1, answer_sem.at[0])
    for load in loads:
        load.wait()
    ext[COUNT, 8:16, :] = jnp.where(mask[...] == 1, count[...], 0).astype(jnp.float32)
    pack_ends(ext, packed)
    start(eastward, lon >= 0)
    greeted = greetings(-1)[1]
    start(westward, greeted)
    start(along, lon >= 0)

    def start_answered(condition):
        @pl.when(condition)
        def _():
            pl.semaphore_wait(answer_sem.at[0], in_column + 1)

        start(westward, condition)

    start_answered(~greeted & last)
    wait_recv(along)
    interior(ext, adj_tracers, adj_east, adj_north, coefs, opens, states, sums)
    pack_strips(ext, own)
    for field in range(STRIPS):
        own_west[field] = turn(own[field], -4)
    start_answered(~greeted & first)
    wait_recv(westward)
    eastern_strip(own, east, adj_tracers, adj_east, adj_north)
    wait_recv(eastward)
    for copy, sent, _ in copies:
        pl.when(sent)(copy.wait_send)


def interior(ext, adj_tracers, adj_east, adj_north, coefs, opens, states, sums):
    ext[COUNT, 7:8, :] = ext[COUNT, 23:24, :]
    ext[COUNT, 24:25, :] = ext[COUNT, 8:9, :]

    def each_level(body):
        def step(level, carry):
            body(level)
            return carry

        lax.fori_loop(0, LEVELS, step, 0, unroll=UNROLL)

    def repeat_ends(level):
        for field in range(8):
            ext[8 * field + level, 7:8, :] = ext[8 * field + level, 23:24, :]
            ext[8 * field + level, 24:25, :] = ext[8 * field + level, 8:9, :]

    each_level(repeat_ends)

    def coefficients(level):
        here = level.astype(jnp.float32)
        cnt = ext[COUNT, 8:24, :]
        vel_e = ext[EAST + level, 8:24, :]
        open_e = jnp.minimum(cnt, turn(cnt, -1)) > here
        open_n = jnp.minimum(cnt, ext[COUNT, 9:25, :]) > here
        made = stencil(
            cnt > here,
            jnp.where(cnt > here + 1.0, VERT, 0.0),
            jnp.where(cnt > here, jnp.where(level > 0, VERT, 0.0), 0.0),
            vel_e,
            turn(vel_e, 1),
            ext[NORTH + level, 8:24, :],
            ext[NORTH + level, 7:23, :],
            open_e,
            jnp.minimum(cnt, turn(cnt, 1)) > here,
            open_n,
            jnp.minimum(cnt, ext[COUNT, 7:23, :]) > here,
        )
        for place, value in enumerate(made):
            coefs[level, place] = value
        opens[level, 0] = jnp.where(open_e[0:8], 0.5, 0.0)
        opens[level, 1] = jnp.where(open_n[0:8], 0.5, 0.0)

    each_level(coefficients)

    def near(source, origin, tracer, level, rows):
        base = origin + LEVELS * tracer
        value = source[base + level, 8 : 8 + rows, :]
        north, south = source[base + level, 9 : 9 + rows, :], source[base + level, 7 : 7 + rows, :]
        above = source[base + jnp.minimum(level + 1, LEVELS - 1), 8 : 8 + rows, :]
        below = source[base + jnp.maximum(level - 1, 0), 8 : 8 + rows, :]
        return value, turn(value, -1), turn(value, 1), north, south, above, below

    def forward_step(step, level):
        source = ext if step == 0 else states
        origin = TRACER if step == 0 else 24 * (step - 1)
        d, e, w, n, s, up, down = (coefs[level, name] for name in FORWARD)
        for tracer in range(TRACERS):
            value, after, before, north, south, above, below = near(source, origin, tracer, level, 16)
            result = d * value - e * after + w * before - n * north + s * south + up * above + down * below
            close_ring(states, 24 * step + LEVELS * tracer + level, result)
            sums[step, 0, LEVELS * tracer + level] = value[:8] + after[:8]
            sums[step, 1, LEVELS * tracer + level] = value[:8] + north[:8]

    def last_sums(level):
        for tracer in range(TRACERS):
            slab = 48 + LEVELS * tracer + level
            value = states[slab, 8:16, :]
            sums[3, 0, LEVELS * tracer + level] = value + turn(value, -1)
            sums[3, 1, LEVELS * tracer + level] = value + states[slab, 9:17, :]

    def adjoint_step(step, level):
        source = ext if step == 0 else states
        origin = COTAN if step == 0 else 24 * (step - 1)
        rows = 16 if step < 3 else 8
        d, e, w, n, s, up, down = (coefs[level, name, :rows] for name in ADJOINT)
        grad_e = jnp.zeros((8, 128), jnp.float32)
        grad_n = jnp.zeros((8, 128), jnp.float32)
        for tracer in range(TRACERS):
            value, after, before, north, south, above, below = near(source, origin, tracer, level, rows)
            result = d * value + e * after - w * before + n * north - s * south + up * above + down * below
            if step < 3:
                close_ring(states, 24 * step + LEVELS * tracer + level, result)
            else:
                adj_tracers[LEVELS * tracer + level] = result
            grad_e = grad_e + sums[3 - step, 0, LEVELS * tracer + level] * (after[:8] - value[:8])
            grad_n = grad_n + sums[3 - step, 1, LEVELS * tracer + level] * (north[:8] - value[:8])
        if step > 0:
            grad_e = grad_e + adj_east[level]
            grad_n = grad_n + adj_north[level]
        if step == 3:
            grad_e = grad_e * opens[level, 0]
            grad_n = grad_n * opens[level, 1]
        adj_east[level] = grad_e
        adj_north[level] = grad_n

    for step in range(3):
        each_level(lambda level, step=step: forward_step(step, level))
    each_level(last_sums)
    for step in range(4):
        each_level(lambda level, step=step: adjoint_step(step, level))


def western_kernel(part_tracers, part_east, part_north, own, west, adj_tracers, adj_east, adj_north):
    lane = lanes_of(16)
    place = lane % 16
    outer = place < 4
    odd = lane % 32 >= 16
    count = own[8]
    for half in range(2):
        for column, field in enumerate(SPARE):
            here = (place == column) & (odd if half else ~odd)
            count = jnp.where(here, turn(west[half], 16 * half + column - HALO * field), count)
    fields = []
    for field in range(8):
        arrived = jnp.where(odd, turn(west[1], 16 - HALO * field), turn(west[0], -HALO * field))
        fields.append(jnp.where(outer, arrived, own[field]))
    parts, targets = (part_tracers, part_east, part_north), (adj_tracers, adj_east, adj_north)
    patch(run_strip(fields, count), parts, targets, -4, lanes_of(8) < 4)


def on_device(tracers, cotangent, east_vel, north_vel, sea_mask, level_count):
    f32 = jnp.float32
    vmem = pl.BlockSpec(memory_space=pltpu.VMEM)
    operands = (tracers.reshape(24, 8, 128), cotangent.reshape(24, 8, 128), east_vel, north_vel, sea_mask, level_count)
    results = (
        jax.ShapeDtypeStruct((24, 8, 128), f32),
        jax.ShapeDtypeStruct((8, 8, 128), f32),
        jax.ShapeDtypeStruct((8, 8, 128), f32),
    )
    parts = pl.pallas_call(
        exchange_kernel,
        name="exchange",
        out_shape=(
            *results,
            jax.ShapeDtypeStruct((STRIPS, 16, 128), f32),
            jax.ShapeDtypeStruct((2, 16, 128), f32),
        ),
        in_specs=[pl.BlockSpec(memory_space=pltpu.HBM)] * 6,
        out_specs=(vmem,) * 5,
        scratch_shapes=[
            pltpu.VMEM((PLANES, ROWS, 128), f32),
            pltpu.VMEM((STRIPS, 16, 128), f32),
            pltpu.VMEM((2, 16, 128), f32),
            pltpu.VMEM((4, 8, 128), f32),
            pltpu.VMEM((8, 128), jnp.int32),
            pltpu.VMEM((8, 128), jnp.int32),
            pltpu.VMEM((LEVELS, 11, 16, 128), f32),
            pltpu.VMEM((LEVELS, 2, 8, 128), f32),
            pltpu.VMEM((72, ROWS, 128), f32),
            pltpu.VMEM((4, 2, 24, 8, 128), f32),
            pltpu.SemaphoreType.DMA((6,)),
            pltpu.SemaphoreType.DMA((8,)),
            pltpu.SemaphoreType.DMA((8,)),
            pltpu.SemaphoreType.REGULAR((1,)),
        ],
        compiler_params=pltpu.CompilerParams(collective_id=0, has_side_effects=True, vmem_limit_bytes=16 << 20),
    )(*(pltpu.with_memory_space_constraint(operand, pltpu.HBM) for operand in operands))
    adj_tracers, adj_east, adj_north = pl.pallas_call(
        western_kernel,
        name="western",
        out_shape=results,
        in_specs=[vmem] * 5,
        out_specs=(vmem,) * 3,
        compiler_params=pltpu.CompilerParams(vmem_limit_bytes=16 << 20),
    )(*parts)
    return adj_tracers.reshape(tracers.shape), adj_east, adj_north


def solution(mesh):
    placed = (
        P(None, None, "lat", "lon"),
        P(None, None, "lat", "lon"),
        P(None, "lat", "lon"),
        P(None, "lat", "lon"),
        P("lat", "lon"),
        P("lat", "lon"),
    )
    return jax.shard_map(
        on_device,
        mesh=mesh,
        in_specs=placed,
        out_specs=(P(None, None, "lat", "lon"), P(None, "lat", "lon"), P(None, "lat", "lon")),
        check_vma=False,
    )
```

```python
import jax
import jax.numpy as jnp
from jax import lax
from jax.experimental import pallas as pl
from jax.experimental.pallas import tpu as pltpu
from jax.sharding import PartitionSpec as P

MESH = pl.DeviceIdType.MESH
HALO = 4
HORIZ = 0.22
VERT = 0.05
LEVELS = 8
TRACERS = 3
UNROLL = 2

TRACER, COTAN, EAST, NORTH, COUNT, PLANES = 0, 24, 48, 56, 64, 65
ROWS = 32
STRIPS = 9
SPARE = (0, 1, 2, 7)
FORWARD = (0, 3, 2, 7, 6, 9, 10)
ADJOINT = (0, 1, 4, 5, 8, 9, 10)


def turn(value, shift):
    return pltpu.roll(value, shift % 128, 1)


def lanes_of(rows):
    return lax.broadcasted_iota(jnp.int32, (rows, 128), 1)


def close_ring(ref, index, value):
    ref[index, 8:24, :] = value
    ref[index, 7:8, :] = value[15:16]
    ref[index, 24:25, :] = value[0:1]


def open_pair(is_open, velocity):
    half = velocity * 0.5
    return jnp.where(is_open, half + HORIZ, 0.0), jnp.where(is_open, half - HORIZ, 0.0)


def stencil(wet, up, down, vel_east, vel_west, vel_north, vel_south, open_east, open_west, open_north, open_south):
    pe, qe = open_pair(open_east, vel_east)
    pw, qw = open_pair(open_west, vel_west)
    pn, qn = open_pair(open_north, vel_north)
    ps, qs = open_pair(open_south, vel_south)
    diagonal = (jnp.where(wet, 1.0, 0.0) - (up + down)) + ((qw - pe) + (qs - pn))
    return diagonal, pe, pw, qe, qw, pn, ps, qn, qs, up, down


def neighbours():
    lat, lon = lax.axis_index("lat"), lax.axis_index("lon")
    last_lat, last_lon = lax.axis_size("lat") - 1, lax.axis_size("lon") - 1
    lats = {0: lat, 1: jnp.where(lat == last_lat, 0, lat + 1), -1: jnp.where(lat == 0, last_lat, lat - 1)}
    lons = {0: lon, 1: jnp.where(lon == last_lon, 0, lon + 1), -1: jnp.where(lon == 0, last_lon, lon - 1)}
    return lambda north, east: {"lat": lats[north], "lon": lons[east]}


def greetings(side):
    place, places = lax.axis_index("lon"), lax.axis_size("lon")
    if places < 3:
        return place >= 0, place >= 0
    if side > 0:
        return (place != places - 1) & (place != places - 2), place >= 0
    return place >= 0, (place != places - 1) & (place != 0)


def pack_last(ext, packed):
    lane = lanes_of(8)
    group = lane // HALO
    counts = ext[COUNT, 8:16, :]
    spread = jnp.zeros((8, 128), jnp.float32)
    for column, field in enumerate(SPARE):
        spread = jnp.where(lane == HALO * field, turn(counts, HALO * field - 124 - column), spread)
    for shift in (32, 64):
        spread = spread + turn(spread, shift)
    is_spare = (lane % 32 == 0) | (lane % 32 == 4) | (lane % 32 == 8) | (lane % 32 == 28)
    for half in range(2):
        last = jnp.zeros((8, 128), jnp.float32)
        for field in range(8):
            for i in range(4):
                place = 8 * i + field
                last = jnp.where(group == place, turn(ext[8 * field + 2 * i + half, 8:16, :], HALO * (place + 1)), last)
        packed[half] = jnp.where(is_spare, spread, last)


def pack_first(ext, packed):
    lane = lanes_of(8)
    group = lane // HALO
    counts = ext[COUNT, 8:16, :]
    for half in range(2):
        first = jnp.zeros((8, 128), jnp.float32)
        for field in range(8):
            for i in range(4):
                place = 8 * i + field
                first = jnp.where(group == (place + 1) % 32, turn(ext[8 * field + 2 * i + half, 8:16, :], HALO * (place + 1)), first)
        if half == 0:
            for i in range(4):
                first = jnp.where(lane == (32 * i + 35) % 128, turn(counts, 31 * i + 35), first)
        packed[2 + half] = first


def pack_strips(ext, own):
    lane = lanes_of(16)
    for field in range(8):
        gathered = jnp.zeros((16, 128), jnp.float32)
        for level in range(LEVELS):
            gathered = jnp.where(lane // 16 == level, turn(ext[8 * field + level, 8:24, :], 16 * level + 8), gathered)
        own[field] = gathered
    gathered = jnp.where(lane < 16, turn(ext[COUNT, 8:24, :], 8), 0.0)
    for shift in (16, 32, 64):
        gathered = gathered + turn(gathered, shift)
    own[8] = gathered


def run_strip(fields, count):
    level = (lanes_of(16) // 16).astype(jnp.float32)

    def north_of(value):
        return pltpu.roll(value, 15, 0)

    def south_of(value):
        return pltpu.roll(value, 1, 0)

    vel_e, vel_n = fields[6], fields[7]
    counts = (count, turn(count, -1), turn(count, 1), north_of(count), south_of(count))
    opened = [jnp.minimum(count, other) > level for other in counts]
    made = stencil(
        opened[0],
        jnp.where(count > level + 1.0, VERT, 0.0),
        jnp.where(opened[0] & (level > 0.0), VERT, 0.0),
        vel_e,
        turn(vel_e, 1),
        vel_n,
        south_of(vel_n),
        *opened[1:],
    )
    opens = [jnp.where(opened[which][:8], 0.5, 0.0) for which in (1, 3)]

    def advanced(value, after, before, north, south, names, rows):
        above, below = turn(value, -16), turn(value, 16)
        d, e, w, n, s, up, down = (made[name][:rows] for name in names)
        value, after, before, north, south, above, below = (item[:rows] for item in (value, after, before, north, south, above, below))
        if names is FORWARD:
            return (d * value - e * after) + (w * before - n * north) + (s * south + (up * above + down * below))
        return (d * value + e * after) + (n * north - w * before) + ((up * above + down * below) - s * south)

    fields = list(fields[:6])
    sums, slopes = {}, {}
    for step in range(4):
        for tracer in range(TRACERS):
            value = fields[tracer]
            after, north = turn(value, -1), north_of(value)
            sums[step, tracer] = ((value + after)[:8], (value + north)[:8])
            if step < 3:
                fields[tracer] = advanced(value, after, turn(value, 1), north, south_of(value), FORWARD, 16)
            value = fields[3 + tracer]
            after, north = turn(value, -1), north_of(value)
            slopes[step, tracer] = ((after - value)[:8], (north - value)[:8])
            fields[3 + tracer] = advanced(value, after, turn(value, 1), north, south_of(value), ADJOINT, 16 if step < 3 else 8)
    grads = []
    for which in range(2):
        total = None
        for step in (1, 2, 0, 3):
            terms = [sums[step, tracer][which] * slopes[3 - step, tracer][which] for tracer in range(TRACERS)]
            part = (terms[0] + terms[1]) + terms[2]
            total = part if total is None else total + part
        grads.append(total * opens[which])
    return fields[3:], grads


def patch(strip, parts, targets, shift, at_end):
    states, grads = strip
    for part, target, base, value in (
        *((parts[0], targets[0], LEVELS * tracer, value) for tracer, value in enumerate(states)),
        (parts[1], targets[1], 0, grads[0]),
        (parts[2], targets[2], 0, grads[1]),
    ):
        for level in range(LEVELS):
            target[base + level] = jnp.where(at_end, turn(value, shift - 16 * level), part[base + level])


def eastern_strip(own, east, adj_tracers, adj_east, adj_north):
    lane = lanes_of(16)
    place = lane % 16
    outer = (place >= 8) & (place < 12)
    odd = lane % 32 >= 16
    fields = []
    for field in range(8):
        arrived = jnp.where(odd, turn(east[1], 20 - 4 * field), turn(east[0], 4 - 4 * field))
        fields.append(jnp.where(outer, arrived, own[field]))
    spread = jnp.zeros((16, 128), jnp.float32)
    for i in range(4):
        spread = jnp.where(lane == 8 + i, turn(east[0], -27 - 31 * i), spread)
    for shift in (16, 32, 64):
        spread = spread + turn(spread, shift)
    parts = (adj_tracers, adj_east, adj_north)
    patch(run_strip(fields, jnp.where(outer, spread, own[8])), parts, parts, 120, lanes_of(8) >= 124)


def exchange_kernel(
    tracers, cotangent, east_vel, north_vel, sea_mask, level_count,
    adj_tracers, adj_east, adj_north, own_west, west,
    ext, own, east, packed, mask, count, coefs, opens, states, sums, load_sem, send_sem, recv_sem, answer_sem,
):
    loads = []
    for source, target in (
        *((tracers.at[at : at + 8], ext.at[TRACER + at : TRACER + at + 8, 8:16, :]) for at in (0, 8, 16)),
        *((cotangent.at[at : at + 8], ext.at[COTAN + at : COTAN + at + 8, 8:16, :]) for at in (0, 8, 16)),
        (east_vel, ext.at[EAST : EAST + 8, 8:16, :]),
        (north_vel, ext.at[NORTH : NORTH + 8, 8:16, :]),
        (sea_mask, mask),
        (level_count, count),
    ):
        loads.append(pltpu.make_async_copy(source, target, load_sem.at[len(loads)]))
        loads[-1].start()

    neighbour = neighbours()
    lat, lats, lon, lons = lax.axis_index("lat"), lax.axis_size("lat"), lax.axis_index("lon"), lax.axis_size("lon")
    exists = {0: lat >= 0, 1: lat < lats - 1, -1: lat > 0}
    barrier = pltpu.get_barrier_semaphore()
    in_column = jnp.where(exists[1], 1, 0) + jnp.where(exists[-1], 1, 0)
    expected = in_column
    for side in (-1, 1):
        greets, greeted = greetings(side)
        expected = expected + jnp.where(greeted, in_column + 1, 0)
        for north in (0, 1, -1):

            @pl.when(greets & exists[north])
            def _():
                pl.semaphore_signal(barrier, inc=1, device_id=neighbour(north, side), device_id_type=MESH)

    for north in (1, -1):

        @pl.when(exists[north])
        def _():
            pl.semaphore_signal(barrier, inc=1, device_id=neighbour(north, 0), device_id_type=MESH)

    for north, rows in ((1, slice(8, 12)), (-1, slice(12, 16))):

        @pl.when(~exists[north])
        def _():
            west[:, rows, :] = jnp.zeros((2, 4, 128), jnp.float32)
            east[:, rows, :] = jnp.zeros((2, 4, 128), jnp.float32)
            ext[:, rows.start + 8 : rows.stop + 8, :] = jnp.zeros((PLANES, 4, 128), jnp.float32)

    west[:, 11:13, :] = jnp.zeros((2, 2, 128), jnp.float32)
    east[:, 11:13, :] = jnp.zeros((2, 2, 128), jnp.float32)
    plan = (
        (1, 1, packed.at[0:2, 5:8, :], west.at[:, 13:16, :]),
        (0, 1, packed.at[0:2], west.at[:, 0:8, :]),
        (-1, 1, packed.at[0:2, 0:3, :], west.at[:, 8:11, :]),
        (0, -1, packed.at[2:4], east.at[:, 0:8, :]),
        (1, -1, packed.at[2:4, 5:8, :], east.at[:, 13:16, :]),
        (-1, -1, packed.at[2:4, 0:3, :], east.at[:, 8:11, :]),
        (1, 0, ext.at[:, 12:16, :], ext.at[:, 20:24, :]),
        (-1, 0, ext.at[:, 8:12, :], ext.at[:, 16:20, :]),
    )
    copies = []
    for north, easterly, source, target in plan:
        copy = pltpu.make_async_remote_copy(
            src_ref=source,
            dst_ref=target,
            send_sem=send_sem.at[len(copies)],
            recv_sem=recv_sem.at[len(copies)],
            device_id=neighbour(north, easterly),
            device_id_type=MESH,
        )
        copies.append((copy, exists[north], exists[-north]))

    def start(chosen, condition):
        for copy, sent, _ in chosen:
            pl.when(sent & condition)(copy.start)

    def wait_recv(chosen):
        for copy, _, received in chosen:
            pl.when(received)(copy.wait_recv)

    def answer(side, theirs):
        for north in (0, 1, -1):

            @pl.when(~greetings(side)[0] & exists[north])
            def _():
                pl.semaphore_signal(theirs, inc=1, device_id=neighbour(north, side), device_id_type=MESH)

    eastward, westward, along = copies[0:3], copies[3:6], copies[6:8]
    first, last = lon == 0, lon == lons - 1
    pl.semaphore_wait(barrier, expected)
    answer(1, answer_sem.at[0])
    for load in loads:
        load.wait()
    ext[COUNT, 8:16, :] = jnp.where(mask[...] == 1, count[...], 0).astype(jnp.float32)
    pack_last(ext, packed)
    start(eastward, lon >= 0)
    pack_first(ext, packed)
    greeted = greetings(-1)[1]
    start(westward, greeted)
    start(along, lon >= 0)

    def start_answered(condition):
        @pl.when(condition)
        def _():
            pl.semaphore_wait(answer_sem.at[0], in_column + 1)

        start(westward, condition)

    start_answered(~greeted & last)
    wait_recv(along)
    interior(ext, adj_tracers, adj_east, adj_north, coefs, opens, states, sums)
    pack_strips(ext, own)
    for field in range(STRIPS):
        own_west[field] = turn(own[field], -4)
    wait_recv(westward)
    eastern_strip(own, east, adj_tracers, adj_east, adj_north)
    start_answered(~greeted & first)
    for copy, sent, _ in copies:
        pl.when(sent)(copy.wait_send)
    wait_recv(eastward)


def interior(ext, adj_tracers, adj_east, adj_north, coefs, opens, states, sums):
    ext[COUNT, 7:8, :] = ext[COUNT, 23:24, :]
    ext[COUNT, 24:25, :] = ext[COUNT, 8:9, :]

    def each_level(body):
        def step(level, carry):
            body(level)
            return carry

        lax.fori_loop(0, LEVELS, step, 0, unroll=UNROLL)

    def repeat_ends(level):
        for field in range(8):
            ext[8 * field + level, 7:8, :] = ext[8 * field + level, 23:24, :]
            ext[8 * field + level, 24:25, :] = ext[8 * field + level, 8:9, :]

    each_level(repeat_ends)

    def coefficients(level):
        here = level.astype(jnp.float32)
        cnt = ext[COUNT, 8:24, :]
        vel_e = ext[EAST + level, 8:24, :]
        open_e = jnp.minimum(cnt, turn(cnt, -1)) > here
        open_n = jnp.minimum(cnt, ext[COUNT, 9:25, :]) > here
        made = stencil(
            cnt > here,
            jnp.where(cnt > here + 1.0, VERT, 0.0),
            jnp.where(cnt > here, jnp.where(level > 0, VERT, 0.0), 0.0),
            vel_e,
            turn(vel_e, 1),
            ext[NORTH + level, 8:24, :],
            ext[NORTH + level, 7:23, :],
            open_e,
            jnp.minimum(cnt, turn(cnt, 1)) > here,
            open_n,
            jnp.minimum(cnt, ext[COUNT, 7:23, :]) > here,
        )
        for place, value in enumerate(made):
            coefs[level, place] = value
        opens[level, 0] = jnp.where(open_e[0:8], 0.5, 0.0)
        opens[level, 1] = jnp.where(open_n[0:8], 0.5, 0.0)

    each_level(coefficients)

    def near(source, origin, tracer, level, rows):
        base = origin + LEVELS * tracer
        value = source[base + level, 8 : 8 + rows, :]
        north, south = source[base + level, 9 : 9 + rows, :], source[base + level, 7 : 7 + rows, :]
        above = source[base + jnp.minimum(level + 1, LEVELS - 1), 8 : 8 + rows, :]
        below = source[base + jnp.maximum(level - 1, 0), 8 : 8 + rows, :]
        return value, turn(value, -1), turn(value, 1), north, south, above, below

    def forward_step(step, level):
        source = ext if step == 0 else states
        origin = TRACER if step == 0 else 24 * (step - 1)
        d, e, w, n, s, up, down = (coefs[level, name] for name in FORWARD)
        for tracer in range(TRACERS):
            value, after, before, north, south, above, below = near(source, origin, tracer, level, 16)
            result = d * value - e * after + w * before - n * north + s * south + up * above + down * below
            close_ring(states, 24 * step + LEVELS * tracer + level, result)
            sums[step, 0, LEVELS * tracer + level] = value[:8] + after[:8]
            sums[step, 1, LEVELS * tracer + level] = value[:8] + north[:8]

    def last_sums(level):
        for tracer in range(TRACERS):
            slab = 48 + LEVELS * tracer + level
            value = states[slab, 8:16, :]
            sums[3, 0, LEVELS * tracer + level] = value + turn(value, -1)
            sums[3, 1, LEVELS * tracer + level] = value + states[slab, 9:17, :]

    def adjoint_step(step, level):
        source = ext if step == 0 else states
        origin = COTAN if step == 0 else 24 * (step - 1)
        rows = 16 if step < 3 else 8
        d, e, w, n, s, up, down = (coefs[level, name, :rows] for name in ADJOINT)
        grad_e = jnp.zeros((8, 128), jnp.float32)
        grad_n = jnp.zeros((8, 128), jnp.float32)
        for tracer in range(TRACERS):
            value, after, before, north, south, above, below = near(source, origin, tracer, level, rows)
            result = d * value + e * after - w * before + n * north - s * south + up * above + down * below
            if step < 3:
                close_ring(states, 24 * step + LEVELS * tracer + level, result)
            else:
                adj_tracers[LEVELS * tracer + level] = result
            grad_e = grad_e + sums[3 - step, 0, LEVELS * tracer + level] * (after[:8] - value[:8])
            grad_n = grad_n + sums[3 - step, 1, LEVELS * tracer + level] * (north[:8] - value[:8])
        if step > 0:
            grad_e = grad_e + adj_east[level]
            grad_n = grad_n + adj_north[level]
        if step == 3:
            grad_e = grad_e * opens[level, 0]
            grad_n = grad_n * opens[level, 1]
        adj_east[level] = grad_e
        adj_north[level] = grad_n

    for step in range(3):
        each_level(lambda level, step=step: forward_step(step, level))
    each_level(last_sums)
    for step in range(4):
        each_level(lambda level, step=step: adjoint_step(step, level))


def western_kernel(part_tracers, part_east, part_north, own, west, adj_tracers, adj_east, adj_north):
    lane = lanes_of(16)
    place = lane % 16
    outer = place < 4
    odd = lane % 32 >= 16
    count = own[8]
    for half in range(2):
        for column, field in enumerate(SPARE):
            here = (place == column) & (odd if half else ~odd)
            count = jnp.where(here, turn(west[half], 16 * half + column - HALO * field), count)
    fields = []
    for field in range(8):
        arrived = jnp.where(odd, turn(west[1], 16 - HALO * field), turn(west[0], -HALO * field))
        fields.append(jnp.where(outer, arrived, own[field]))
    parts, targets = (part_tracers, part_east, part_north), (adj_tracers, adj_east, adj_north)
    patch(run_strip(fields, count), parts, targets, -4, lanes_of(8) < 4)


def on_device(tracers, cotangent, east_vel, north_vel, sea_mask, level_count):
    f32 = jnp.float32
    vmem = pl.BlockSpec(memory_space=pltpu.VMEM)
    operands = (tracers.reshape(24, 8, 128), cotangent.reshape(24, 8, 128), east_vel, north_vel, sea_mask, level_count)
    results = (
        jax.ShapeDtypeStruct((24, 8, 128), f32),
        jax.ShapeDtypeStruct((8, 8, 128), f32),
        jax.ShapeDtypeStruct((8, 8, 128), f32),
    )
    parts = pl.pallas_call(
        exchange_kernel,
        name="exchange",
        out_shape=(
            *results,
            jax.ShapeDtypeStruct((STRIPS, 16, 128), f32),
            jax.ShapeDtypeStruct((2, 16, 128), f32),
        ),
        in_specs=[pl.BlockSpec(memory_space=pltpu.HBM)] * 6,
        out_specs=(vmem,) * 5,
        scratch_shapes=[
            pltpu.VMEM((PLANES, ROWS, 128), f32),
            pltpu.VMEM((STRIPS, 16, 128), f32),
            pltpu.VMEM((2, 16, 128), f32),
            pltpu.VMEM((4, 8, 128), f32),
            pltpu.VMEM((8, 128), jnp.int32),
            pltpu.VMEM((8, 128), jnp.int32),
            pltpu.VMEM((LEVELS, 11, 16, 128), f32),
            pltpu.VMEM((LEVELS, 2, 8, 128), f32),
            pltpu.VMEM((72, ROWS, 128), f32),
            pltpu.VMEM((4, 2, 24, 8, 128), f32),
            pltpu.SemaphoreType.DMA((10,)),
            pltpu.SemaphoreType.DMA((8,)),
            pltpu.SemaphoreType.DMA((8,)),
            pltpu.SemaphoreType.REGULAR((1,)),
        ],
        compiler_params=pltpu.CompilerParams(collective_id=0, has_side_effects=True, vmem_limit_bytes=16 << 20),
    )(*(pltpu.with_memory_space_constraint(operand, pltpu.HBM) for operand in operands))
    adj_tracers, adj_east, adj_north = pl.pallas_call(
        western_kernel,
        name="western",
        out_shape=results,
        in_specs=[vmem] * 5,
        out_specs=(vmem,) * 3,
        compiler_params=pltpu.CompilerParams(vmem_limit_bytes=16 << 20),
    )(*parts)
    return adj_tracers.reshape(tracers.shape), adj_east, adj_north


def solution(mesh):
    placed = (
        P(None, None, "lat", "lon"),
        P(None, None, "lat", "lon"),
        P(None, "lat", "lon"),
        P(None, "lat", "lon"),
        P("lat", "lon"),
        P("lat", "lon"),
    )
    return jax.shard_map(
        on_device,
        mesh=mesh,
        in_specs=placed,
        out_specs=(P(None, None, "lat", "lon"), P(None, "lat", "lon"), P(None, "lat", "lon")),
        check_vma=False,
    )
```

```python
import jax
import jax.numpy as jnp
from jax import lax
from jax.experimental import pallas as pl
from jax.experimental.pallas import tpu as pltpu
from jax.sharding import PartitionSpec as P

MESH = pl.DeviceIdType.MESH
HALO = 4
HORIZ = 0.22
VERT = 0.05
LEVELS = 8
TRACERS = 3
UNROLL = 2

TRACER, COTAN, EAST, NORTH, COUNT, PLANES = 0, 24, 48, 56, 64, 65
ROWS = 32
STRIPS = 9
SPARE = (0, 1, 2, 7)
FORWARD = (0, 3, 2, 7, 6, 9, 10)
ADJOINT = (0, 1, 4, 5, 8, 9, 10)


def turn(value, shift):
    return pltpu.roll(value, shift % 128, 1)


def lanes_of(rows):
    return lax.broadcasted_iota(jnp.int32, (rows, 128), 1)


def close_ring(ref, index, value):
    ref[index, 8:24, :] = value
    ref[index, 7:8, :] = value[15:16]
    ref[index, 24:25, :] = value[0:1]


def open_pair(is_open, velocity):
    half = velocity * 0.5
    return jnp.where(is_open, half + HORIZ, 0.0), jnp.where(is_open, half - HORIZ, 0.0)


def stencil(wet, up, down, vel_east, vel_west, vel_north, vel_south, open_east, open_west, open_north, open_south):
    pe, qe = open_pair(open_east, vel_east)
    pw, qw = open_pair(open_west, vel_west)
    pn, qn = open_pair(open_north, vel_north)
    ps, qs = open_pair(open_south, vel_south)
    diagonal = (jnp.where(wet, 1.0, 0.0) - (up + down)) + ((qw - pe) + (qs - pn))
    return diagonal, pe, pw, qe, qw, pn, ps, qn, qs, up, down


def neighbours():
    lat, lon = lax.axis_index("lat"), lax.axis_index("lon")
    last_lat, last_lon = lax.axis_size("lat") - 1, lax.axis_size("lon") - 1
    lats = {0: lat, 1: jnp.where(lat == last_lat, 0, lat + 1), -1: jnp.where(lat == 0, last_lat, lat - 1)}
    lons = {0: lon, 1: jnp.where(lon == last_lon, 0, lon + 1), -1: jnp.where(lon == 0, last_lon, lon - 1)}
    return lambda north, east: {"lat": lats[north], "lon": lons[east]}


def greetings(side):
    place, places = lax.axis_index("lon"), lax.axis_size("lon")
    if places < 3:
        return place >= 0, place >= 0
    if side > 0:
        return (place != places - 1) & (place != places - 2), place >= 0
    return place >= 0, (place != places - 1) & (place != 0)


def pack_last(ext, packed):
    lane = lanes_of(8)
    group = lane // HALO
    counts = ext[COUNT, 8:16, :]
    spread = jnp.zeros((8, 128), jnp.float32)
    for column, field in enumerate(SPARE):
        spread = jnp.where(lane == HALO * field, turn(counts, HALO * field - 124 - column), spread)
    for shift in (32, 64):
        spread = spread + turn(spread, shift)
    is_spare = (lane % 32 == 0) | (lane % 32 == 4) | (lane % 32 == 8) | (lane % 32 == 28)
    for half in range(2):
        last = jnp.zeros((8, 128), jnp.float32)
        for field in range(8):
            for i in range(4):
                place = 8 * i + field
                last = jnp.where(group == place, turn(ext[8 * field + 2 * i + half, 8:16, :], HALO * (place + 1)), last)
        packed[half] = jnp.where(is_spare, spread, last)


def pack_first(ext, packed):
    lane = lanes_of(8)
    group = lane // HALO
    counts = ext[COUNT, 8:16, :]
    for half in range(2):
        first = jnp.zeros((8, 128), jnp.float32)
        for field in range(8):
            for i in range(4):
                place = 8 * i + field
                first = jnp.where(group == (place + 1) % 32, turn(ext[8 * field + 2 * i + half, 8:16, :], HALO * (place + 1)), first)
        if half == 0:
            for i in range(4):
                first = jnp.where(lane == (32 * i + 35) % 128, turn(counts, 31 * i + 35), first)
        packed[2 + half] = first


def pack_strips(ext, own):
    lane = lanes_of(16)
    for field in range(8):
        gathered = jnp.zeros((16, 128), jnp.float32)
        for level in range(LEVELS):
            gathered = jnp.where(lane // 16 == level, turn(ext[8 * field + level, 8:24, :], 16 * level + 8), gathered)
        own[field] = gathered
    gathered = jnp.where(lane < 16, turn(ext[COUNT, 8:24, :], 8), 0.0)
    for shift in (16, 32, 64):
        gathered = gathered + turn(gathered, shift)
    own[8] = gathered


def run_strip(fields, count):
    level = (lanes_of(16) // 16).astype(jnp.float32)

    def north_of(value):
        return pltpu.roll(value, 15, 0)

    def south_of(value):
        return pltpu.roll(value, 1, 0)

    vel_e, vel_n = fields[6], fields[7]
    counts = (count, turn(count, -1), turn(count, 1), north_of(count), south_of(count))
    opened = [jnp.minimum(count, other) > level for other in counts]
    made = stencil(
        opened[0],
        jnp.where(count > level + 1.0, VERT, 0.0),
        jnp.where(opened[0] & (level > 0.0), VERT, 0.0),
        vel_e,
        turn(vel_e, 1),
        vel_n,
        south_of(vel_n),
        *opened[1:],
    )
    opens = [jnp.where(opened[which][:8], 0.5, 0.0) for which in (1, 3)]

    def advanced(value, after, before, north, south, names, rows):
        above, below = turn(value, -16), turn(value, 16)
        d, e, w, n, s, up, down = (made[name][:rows] for name in names)
        value, after, before, north, south, above, below = (item[:rows] for item in (value, after, before, north, south, above, below))
        if names is FORWARD:
            return (d * value - e * after) + (w * before - n * north) + (s * south + (up * above + down * below))
        return (d * value + e * after) + (n * north - w * before) + ((up * above + down * below) - s * south)

    fields = list(fields[:6])
    sums, slopes = {}, {}
    for step in range(4):
        for tracer in range(TRACERS):
            value = fields[tracer]
            after, north = turn(value, -1), north_of(value)
            sums[step, tracer] = ((value + after)[:8], (value + north)[:8])
            if step < 3:
                fields[tracer] = advanced(value, after, turn(value, 1), north, south_of(value), FORWARD, 16)
            value = fields[3 + tracer]
            after, north = turn(value, -1), north_of(value)
            slopes[step, tracer] = ((after - value)[:8], (north - value)[:8])
            fields[3 + tracer] = advanced(value, after, turn(value, 1), north, south_of(value), ADJOINT, 16 if step < 3 else 8)
    grads = []
    for which in range(2):
        total = None
        for step in (1, 2, 0, 3):
            terms = [sums[step, tracer][which] * slopes[3 - step, tracer][which] for tracer in range(TRACERS)]
            part = (terms[0] + terms[1]) + terms[2]
            total = part if total is None else total + part
        grads.append(total * opens[which])
    return fields[3:], grads


def patch(strip, parts, targets, shift, at_end):
    states, grads = strip
    for part, target, base, value in (
        *((parts[0], targets[0], LEVELS * tracer, value) for tracer, value in enumerate(states)),
        (parts[1], targets[1], 0, grads[0]),
        (parts[2], targets[2], 0, grads[1]),
    ):
        for level in range(LEVELS):
            target[base + level] = jnp.where(at_end, turn(value, shift - 16 * level), part[base + level])


def eastern_strip(own, east, adj_tracers, adj_east, adj_north):
    lane = lanes_of(16)
    place = lane % 16
    outer = (place >= 8) & (place < 12)
    odd = lane % 32 >= 16
    fields = []
    for field in range(8):
        arrived = jnp.where(odd, turn(east[1], 20 - 4 * field), turn(east[0], 4 - 4 * field))
        fields.append(jnp.where(outer, arrived, own[field]))
    spread = jnp.zeros((16, 128), jnp.float32)
    for i in range(4):
        spread = jnp.where(lane == 8 + i, turn(east[0], -27 - 31 * i), spread)
    for shift in (16, 32, 64):
        spread = spread + turn(spread, shift)
    parts = (adj_tracers, adj_east, adj_north)
    patch(run_strip(fields, jnp.where(outer, spread, own[8])), parts, parts, 120, lanes_of(8) >= 124)


def exchange_kernel(
    tracers, cotangent, east_vel, north_vel, sea_mask, level_count,
    adj_tracers, adj_east, adj_north, own_west, west,
    ext, own, east, packed, mask, count, coefs, opens, states, sums, load_sem, send_sem, recv_sem, answer_sem,
):
    loads = []
    for source, target in (
        *((tracers.at[at : at + 8], ext.at[TRACER + at : TRACER + at + 8, 8:16, :]) for at in (0, 8, 16)),
        *((cotangent.at[at : at + 8], ext.at[COTAN + at : COTAN + at + 8, 8:16, :]) for at in (0, 8, 16)),
        (east_vel, ext.at[EAST : EAST + 8, 8:16, :]),
        (north_vel, ext.at[NORTH : NORTH + 8, 8:16, :]),
        (sea_mask, mask),
        (level_count, count),
    ):
        loads.append(pltpu.make_async_copy(source, target, load_sem.at[len(loads)]))
        loads[-1].start()

    neighbour = neighbours()
    lat, lats, lon, lons = lax.axis_index("lat"), lax.axis_size("lat"), lax.axis_index("lon"), lax.axis_size("lon")
    exists = {0: lat >= 0, 1: lat < lats - 1, -1: lat > 0}
    barrier = pltpu.get_barrier_semaphore()
    in_column = jnp.where(exists[1], 1, 0) + jnp.where(exists[-1], 1, 0)
    expected = in_column
    for side in (-1, 1):
        greets, greeted = greetings(side)
        expected = expected + jnp.where(greeted, in_column + 1, 0)
        for north in (0, 1, -1):

            @pl.when(greets & exists[north])
            def _():
                pl.semaphore_signal(barrier, inc=1, device_id=neighbour(north, side), device_id_type=MESH)

    for north in (1, -1):

        @pl.when(exists[north])
        def _():
            pl.semaphore_signal(barrier, inc=1, device_id=neighbour(north, 0), device_id_type=MESH)

    for north, rows in ((1, slice(8, 12)), (-1, slice(12, 16))):

        @pl.when(~exists[north])
        def _():
            west[:, rows, :] = jnp.zeros((2, 4, 128), jnp.float32)
            east[:, rows, :] = jnp.zeros((2, 4, 128), jnp.float32)
            ext[:, rows.start + 8 : rows.stop + 8, :] = jnp.zeros((PLANES, 4, 128), jnp.float32)

    west[:, 11:13, :] = jnp.zeros((2, 2, 128), jnp.float32)
    east[:, 11:13, :] = jnp.zeros((2, 2, 128), jnp.float32)
    plan = (
        (1, 1, packed.at[0:2, 5:8, :], west.at[:, 13:16, :]),
        (0, 1, packed.at[0:2], west.at[:, 0:8, :]),
        (-1, 1, packed.at[0:2, 0:3, :], west.at[:, 8:11, :]),
        (0, -1, packed.at[2:4], east.at[:, 0:8, :]),
        (1, -1, packed.at[2:4, 5:8, :], east.at[:, 13:16, :]),
        (-1, -1, packed.at[2:4, 0:3, :], east.at[:, 8:11, :]),
        (1, 0, ext.at[:, 12:16, :], ext.at[:, 20:24, :]),
        (-1, 0, ext.at[:, 8:12, :], ext.at[:, 16:20, :]),
    )
    copies = []
    for north, easterly, source, target in plan:
        copy = pltpu.make_async_remote_copy(
            src_ref=source,
            dst_ref=target,
            send_sem=send_sem.at[len(copies)],
            recv_sem=recv_sem.at[len(copies)],
            device_id=neighbour(north, easterly),
            device_id_type=MESH,
        )
        copies.append((copy, exists[north], exists[-north]))

    def start(chosen, condition):
        for copy, sent, _ in chosen:
            pl.when(sent & condition)(copy.start)

    def wait_recv(chosen):
        for copy, _, received in chosen:
            pl.when(received)(copy.wait_recv)

    def answer(side, theirs):
        for north in (0, 1, -1):

            @pl.when(~greetings(side)[0] & exists[north])
            def _():
                pl.semaphore_signal(theirs, inc=1, device_id=neighbour(north, side), device_id_type=MESH)

    eastward, westward, along = copies[0:3], copies[3:6], copies[6:8]
    first, last = lon == 0, lon == lons - 1
    for load in loads:
        load.wait()
    ext[COUNT, 8:16, :] = jnp.where(mask[...] == 1, count[...], 0).astype(jnp.float32)
    pack_last(ext, packed)
    pl.semaphore_wait(barrier, expected)
    start(eastward, lon >= 0)
    answer(1, answer_sem.at[0])
    pack_first(ext, packed)
    greeted = greetings(-1)[1]
    start(westward, greeted)
    start(along, lon >= 0)

    def start_answered(condition):
        @pl.when(condition)
        def _():
            pl.semaphore_wait(answer_sem.at[0], in_column + 1)

        start(westward, condition)

    start_answered(~greeted & last)
    wait_recv(along)
    interior(ext, adj_tracers, adj_east, adj_north, coefs, opens, states, sums)
    pack_strips(ext, own)
    for field in range(STRIPS):
        own_west[field] = turn(own[field], -4)
    wait_recv(westward)
    eastern_strip(own, east, adj_tracers, adj_east, adj_north)
    start_answered(~greeted & first)
    for copy, sent, _ in copies:
        pl.when(sent)(copy.wait_send)
    wait_recv(eastward)


def interior(ext, adj_tracers, adj_east, adj_north, coefs, opens, states, sums):
    ext[COUNT, 7:8, :] = ext[COUNT, 23:24, :]
    ext[COUNT, 24:25, :] = ext[COUNT, 8:9, :]

    def each_level(body):
        def step(level, carry):
            body(level)
            return carry

        lax.fori_loop(0, LEVELS, step, 0, unroll=UNROLL)

    def repeat_ends(level):
        for field in range(8):
            ext[8 * field + level, 7:8, :] = ext[8 * field + level, 23:24, :]
            ext[8 * field + level, 24:25, :] = ext[8 * field + level, 8:9, :]

    each_level(repeat_ends)

    def coefficients(level):
        here = level.astype(jnp.float32)
        cnt = ext[COUNT, 8:24, :]
        vel_e = ext[EAST + level, 8:24, :]
        open_e = jnp.minimum(cnt, turn(cnt, -1)) > here
        open_n = jnp.minimum(cnt, ext[COUNT, 9:25, :]) > here
        made = stencil(
            cnt > here,
            jnp.where(cnt > here + 1.0, VERT, 0.0),
            jnp.where(cnt > here, jnp.where(level > 0, VERT, 0.0), 0.0),
            vel_e,
            turn(vel_e, 1),
            ext[NORTH + level, 8:24, :],
            ext[NORTH + level, 7:23, :],
            open_e,
            jnp.minimum(cnt, turn(cnt, 1)) > here,
            open_n,
            jnp.minimum(cnt, ext[COUNT, 7:23, :]) > here,
        )
        for place, value in enumerate(made):
            coefs[level, place] = value
        opens[level, 0] = jnp.where(open_e[0:8], 0.5, 0.0)
        opens[level, 1] = jnp.where(open_n[0:8], 0.5, 0.0)

    each_level(coefficients)

    def near(source, origin, tracer, level, rows):
        base = origin + LEVELS * tracer
        value = source[base + level, 8 : 8 + rows, :]
        north, south = source[base + level, 9 : 9 + rows, :], source[base + level, 7 : 7 + rows, :]
        above = source[base + jnp.minimum(level + 1, LEVELS - 1), 8 : 8 + rows, :]
        below = source[base + jnp.maximum(level - 1, 0), 8 : 8 + rows, :]
        return value, turn(value, -1), turn(value, 1), north, south, above, below

    def forward_step(step, level):
        source = ext if step == 0 else states
        origin = TRACER if step == 0 else 24 * (step - 1)
        d, e, w, n, s, up, down = (coefs[level, name] for name in FORWARD)
        for tracer in range(TRACERS):
            value, after, before, north, south, above, below = near(source, origin, tracer, level, 16)
            result = d * value - e * after + w * before - n * north + s * south + up * above + down * below
            close_ring(states, 24 * step + LEVELS * tracer + level, result)
            sums[step, 0, LEVELS * tracer + level] = value[:8] + after[:8]
            sums[step, 1, LEVELS * tracer + level] = value[:8] + north[:8]

    def last_sums(level):
        for tracer in range(TRACERS):
            slab = 48 + LEVELS * tracer + level
            value = states[slab, 8:16, :]
            sums[3, 0, LEVELS * tracer + level] = value + turn(value, -1)
            sums[3, 1, LEVELS * tracer + level] = value + states[slab, 9:17, :]

    def adjoint_step(step, level):
        source = ext if step == 0 else states
        origin = COTAN if step == 0 else 24 * (step - 1)
        rows = 16 if step < 3 else 8
        d, e, w, n, s, up, down = (coefs[level, name, :rows] for name in ADJOINT)
        grad_e = jnp.zeros((8, 128), jnp.float32)
        grad_n = jnp.zeros((8, 128), jnp.float32)
        for tracer in range(TRACERS):
            value, after, before, north, south, above, below = near(source, origin, tracer, level, rows)
            result = d * value + e * after - w * before + n * north - s * south + up * above + down * below
            if step < 3:
                close_ring(states, 24 * step + LEVELS * tracer + level, result)
            else:
                adj_tracers[LEVELS * tracer + level] = result
            grad_e = grad_e + sums[3 - step, 0, LEVELS * tracer + level] * (after[:8] - value[:8])
            grad_n = grad_n + sums[3 - step, 1, LEVELS * tracer + level] * (north[:8] - value[:8])
        if step > 0:
            grad_e = grad_e + adj_east[level]
            grad_n = grad_n + adj_north[level]
        if step == 3:
            grad_e = grad_e * opens[level, 0]
            grad_n = grad_n * opens[level, 1]
        adj_east[level] = grad_e
        adj_north[level] = grad_n

    for step in range(3):
        each_level(lambda level, step=step: forward_step(step, level))
    each_level(last_sums)
    for step in range(4):
        each_level(lambda level, step=step: adjoint_step(step, level))


def western_kernel(part_tracers, part_east, part_north, own, west, adj_tracers, adj_east, adj_north):
    lane = lanes_of(16)
    place = lane % 16
    outer = place < 4
    odd = lane % 32 >= 16
    count = own[8]
    for half in range(2):
        for column, field in enumerate(SPARE):
            here = (place == column) & (odd if half else ~odd)
            count = jnp.where(here, turn(west[half], 16 * half + column - HALO * field), count)
    fields = []
    for field in range(8):
        arrived = jnp.where(odd, turn(west[1], 16 - HALO * field), turn(west[0], -HALO * field))
        fields.append(jnp.where(outer, arrived, own[field]))
    parts, targets = (part_tracers, part_east, part_north), (adj_tracers, adj_east, adj_north)
    patch(run_strip(fields, count), parts, targets, -4, lanes_of(8) < 4)


def on_device(tracers, cotangent, east_vel, north_vel, sea_mask, level_count):
    f32 = jnp.float32
    vmem = pl.BlockSpec(memory_space=pltpu.VMEM)
    operands = (tracers.reshape(24, 8, 128), cotangent.reshape(24, 8, 128), east_vel, north_vel, sea_mask, level_count)
    results = (
        jax.ShapeDtypeStruct((24, 8, 128), f32),
        jax.ShapeDtypeStruct((8, 8, 128), f32),
        jax.ShapeDtypeStruct((8, 8, 128), f32),
    )
    parts = pl.pallas_call(
        exchange_kernel,
        name="exchange",
        out_shape=(
            *results,
            jax.ShapeDtypeStruct((STRIPS, 16, 128), f32),
            jax.ShapeDtypeStruct((2, 16, 128), f32),
        ),
        in_specs=[pl.BlockSpec(memory_space=pltpu.HBM)] * 6,
        out_specs=(vmem,) * 5,
        scratch_shapes=[
            pltpu.VMEM((PLANES, ROWS, 128), f32),
            pltpu.VMEM((STRIPS, 16, 128), f32),
            pltpu.VMEM((2, 16, 128), f32),
            pltpu.VMEM((4, 8, 128), f32),
            pltpu.VMEM((8, 128), jnp.int32),
            pltpu.VMEM((8, 128), jnp.int32),
            pltpu.VMEM((LEVELS, 11, 16, 128), f32),
            pltpu.VMEM((LEVELS, 2, 8, 128), f32),
            pltpu.VMEM((72, ROWS, 128), f32),
            pltpu.VMEM((4, 2, 24, 8, 128), f32),
            pltpu.SemaphoreType.DMA((10,)),
            pltpu.SemaphoreType.DMA((8,)),
            pltpu.SemaphoreType.DMA((8,)),
            pltpu.SemaphoreType.REGULAR((1,)),
        ],
        compiler_params=pltpu.CompilerParams(collective_id=0, has_side_effects=True, vmem_limit_bytes=16 << 20),
    )(*(pltpu.with_memory_space_constraint(operand, pltpu.HBM) for operand in operands))
    adj_tracers, adj_east, adj_north = pl.pallas_call(
        western_kernel,
        name="western",
        out_shape=results,
        in_specs=[vmem] * 5,
        out_specs=(vmem,) * 3,
        compiler_params=pltpu.CompilerParams(vmem_limit_bytes=16 << 20),
    )(*parts)
    return adj_tracers.reshape(tracers.shape), adj_east, adj_north


def solution(mesh):
    placed = (
        P(None, None, "lat", "lon"),
        P(None, None, "lat", "lon"),
        P(None, "lat", "lon"),
        P(None, "lat", "lon"),
        P("lat", "lon"),
        P("lat", "lon"),
    )
    return jax.shard_map(
        on_device,
        mesh=mesh,
        in_specs=placed,
        out_specs=(P(None, None, "lat", "lon"), P(None, "lat", "lon"), P(None, "lat", "lon")),
        check_vma=False,
    )
```

```python
import jax
import jax.numpy as jnp
from jax import lax
from jax.experimental import pallas as pl
from jax.experimental.pallas import tpu as pltpu
from jax.sharding import PartitionSpec as P

MESH = pl.DeviceIdType.MESH
HALO = 4
HORIZ = 0.22
VERT = 0.05
LEVELS = 8
TRACERS = 3
UNROLL = 2

TRACER, COTAN, EAST, NORTH, COUNT, PLANES = 0, 24, 48, 56, 64, 65
ROWS = 32
STRIPS = 9
SPARE = (0, 1, 2, 7)
FORWARD = (0, 3, 2, 7, 6, 9, 10)
ADJOINT = (0, 1, 4, 5, 8, 9, 10)


def turn(value, shift):
    return pltpu.roll(value, shift % 128, 1)


def lanes_of(rows):
    return lax.broadcasted_iota(jnp.int32, (rows, 128), 1)


def close_ring(ref, index, value):
    ref[index, 8:24, :] = value
    ref[index, 7:8, :] = value[15:16]
    ref[index, 24:25, :] = value[0:1]


def open_pair(is_open, velocity):
    half = velocity * 0.5
    return jnp.where(is_open, half + HORIZ, 0.0), jnp.where(is_open, half - HORIZ, 0.0)


def stencil(wet, up, down, vel_east, vel_west, vel_north, vel_south, open_east, open_west, open_north, open_south):
    pe, qe = open_pair(open_east, vel_east)
    pw, qw = open_pair(open_west, vel_west)
    pn, qn = open_pair(open_north, vel_north)
    ps, qs = open_pair(open_south, vel_south)
    diagonal = (jnp.where(wet, 1.0, 0.0) - (up + down)) + ((qw - pe) + (qs - pn))
    return diagonal, pe, pw, qe, qw, pn, ps, qn, qs, up, down


def neighbours():
    lat, lon = lax.axis_index("lat"), lax.axis_index("lon")
    last_lat, last_lon = lax.axis_size("lat") - 1, lax.axis_size("lon") - 1
    lats = {0: lat, 1: jnp.where(lat == last_lat, 0, lat + 1), -1: jnp.where(lat == 0, last_lat, lat - 1)}
    lons = {0: lon, 1: jnp.where(lon == last_lon, 0, lon + 1), -1: jnp.where(lon == 0, last_lon, lon - 1)}
    return lambda north, east: {"lat": lats[north], "lon": lons[east]}


def greetings(side):
    place, places = lax.axis_index("lon"), lax.axis_size("lon")
    if places < 3:
        return place >= 0, place >= 0
    if side > 0:
        return (place != places - 1) & (place != places - 2), place >= 0
    return place >= 0, (place != places - 1) & (place != 0)


def pack_last(ext, packed):
    lane = lanes_of(8)
    group = lane // HALO
    counts = ext[COUNT, 8:16, :]
    spread = jnp.zeros((8, 128), jnp.float32)
    for column, field in enumerate(SPARE):
        spread = jnp.where(lane == HALO * field, turn(counts, HALO * field - 124 - column), spread)
    for shift in (32, 64):
        spread = spread + turn(spread, shift)
    is_spare = (lane % 32 == 0) | (lane % 32 == 4) | (lane % 32 == 8) | (lane % 32 == 28)
    for half in range(2):
        last = jnp.zeros((8, 128), jnp.float32)
        for field in range(8):
            for i in range(4):
                place = 8 * i + field
                last = jnp.where(group == place, turn(ext[8 * field + 2 * i + half, 8:16, :], HALO * (place + 1)), last)
        packed[half] = jnp.where(is_spare, spread, last)


def pack_first(ext, packed):
    lane = lanes_of(8)
    group = lane // HALO
    counts = ext[COUNT, 8:16, :]
    for half in range(2):
        first = jnp.zeros((8, 128), jnp.float32)
        for field in range(8):
            for i in range(4):
                place = 8 * i + field
                first = jnp.where(group == (place + 1) % 32, turn(ext[8 * field + 2 * i + half, 8:16, :], HALO * (place + 1)), first)
        if half == 0:
            for i in range(4):
                first = jnp.where(lane == (32 * i + 35) % 128, turn(counts, 31 * i + 35), first)
        packed[2 + half] = first


def pack_strips(ext, own):
    lane = lanes_of(16)
    for field in range(8):
        gathered = jnp.zeros((16, 128), jnp.float32)
        for level in range(LEVELS):
            gathered = jnp.where(lane // 16 == level, turn(ext[8 * field + level, 8:24, :], 16 * level + 8), gathered)
        own[field] = gathered
    gathered = jnp.where(lane < 16, turn(ext[COUNT, 8:24, :], 8), 0.0)
    for shift in (16, 32, 64):
        gathered = gathered + turn(gathered, shift)
    own[8] = gathered


def run_strip(fields, count):
    level = (lanes_of(16) // 16).astype(jnp.float32)

    def north_of(value):
        return pltpu.roll(value, 15, 0)

    def south_of(value):
        return pltpu.roll(value, 1, 0)

    vel_e, vel_n = fields[6], fields[7]
    counts = (count, turn(count, -1), turn(count, 1), north_of(count), south_of(count))
    opened = [jnp.minimum(count, other) > level for other in counts]
    made = stencil(
        opened[0],
        jnp.where(count > level + 1.0, VERT, 0.0),
        jnp.where(opened[0] & (level > 0.0), VERT, 0.0),
        vel_e,
        turn(vel_e, 1),
        vel_n,
        south_of(vel_n),
        *opened[1:],
    )
    opens = [jnp.where(opened[which][:8], 0.5, 0.0) for which in (1, 3)]

    def advanced(value, after, before, north, south, names, rows):
        above, below = turn(value, -16), turn(value, 16)
        d, e, w, n, s, up, down = (made[name][:rows] for name in names)
        value, after, before, north, south, above, below = (item[:rows] for item in (value, after, before, north, south, above, below))
        if names is FORWARD:
            return (d * value - e * after) + (w * before - n * north) + (s * south + (up * above + down * below))
        return (d * value + e * after) + (n * north - w * before) + ((up * above + down * below) - s * south)

    fields = list(fields[:6])
    sums, slopes = {}, {}
    for step in range(4):
        for tracer in range(TRACERS):
            value = fields[tracer]
            after, north = turn(value, -1), north_of(value)
            sums[step, tracer] = ((value + after)[:8], (value + north)[:8])
            if step < 3:
                fields[tracer] = advanced(value, after, turn(value, 1), north, south_of(value), FORWARD, 16)
            value = fields[3 + tracer]
            after, north = turn(value, -1), north_of(value)
            slopes[step, tracer] = ((after - value)[:8], (north - value)[:8])
            fields[3 + tracer] = advanced(value, after, turn(value, 1), north, south_of(value), ADJOINT, 16 if step < 3 else 8)
    grads = []
    for which in range(2):
        total = None
        for step in (1, 2, 0, 3):
            terms = [sums[step, tracer][which] * slopes[3 - step, tracer][which] for tracer in range(TRACERS)]
            part = (terms[0] + terms[1]) + terms[2]
            total = part if total is None else total + part
        grads.append(total * opens[which])
    return fields[3:], grads


def patch(strip, parts, targets, shift, at_end):
    states, grads = strip
    for part, target, base, value in (
        *((parts[0], targets[0], LEVELS * tracer, value) for tracer, value in enumerate(states)),
        (parts[1], targets[1], 0, grads[0]),
        (parts[2], targets[2], 0, grads[1]),
    ):
        for level in range(LEVELS):
            target[base + level] = jnp.where(at_end, turn(value, shift - 16 * level), part[base + level])


def eastern_strip(own, east, adj_tracers, adj_east, adj_north):
    lane = lanes_of(16)
    place = lane % 16
    outer = (place >= 8) & (place < 12)
    odd = lane % 32 >= 16
    fields = []
    for field in range(8):
        arrived = jnp.where(odd, turn(east[1], 20 - 4 * field), turn(east[0], 4 - 4 * field))
        fields.append(jnp.where(outer, arrived, own[field]))
    spread = jnp.zeros((16, 128), jnp.float32)
    for i in range(4):
        spread = jnp.where(lane == 8 + i, turn(east[0], -27 - 31 * i), spread)
    for shift in (16, 32, 64):
        spread = spread + turn(spread, shift)
    parts = (adj_tracers, adj_east, adj_north)
    patch(run_strip(fields, jnp.where(outer, spread, own[8])), parts, parts, 120, lanes_of(8) >= 124)


def exchange_kernel(
    tracers, cotangent, east_vel, north_vel, sea_mask, level_count,
    adj_tracers, adj_east, adj_north, own_west, west,
    ext, own, east, packed, mask, count, coefs, opens, states, sums, load_sem, send_sem, recv_sem, answer_sem, told_sem,
):
    loads = []
    for source, target in (
        *((tracers.at[at : at + 8], ext.at[TRACER + at : TRACER + at + 8, 8:16, :]) for at in (0, 8, 16)),
        *((cotangent.at[at : at + 8], ext.at[COTAN + at : COTAN + at + 8, 8:16, :]) for at in (0, 8, 16)),
        (east_vel, ext.at[EAST : EAST + 8, 8:16, :]),
        (north_vel, ext.at[NORTH : NORTH + 8, 8:16, :]),
        (sea_mask, mask),
        (level_count, count),
    ):
        loads.append(pltpu.make_async_copy(source, target, load_sem.at[len(loads)]))
        loads[-1].start()

    neighbour = neighbours()
    lat, lats, lon, lons = lax.axis_index("lat"), lax.axis_size("lat"), lax.axis_index("lon"), lax.axis_size("lon")
    exists = {0: lat >= 0, 1: lat < lats - 1, -1: lat > 0}
    barrier = pltpu.get_barrier_semaphore()
    in_column = jnp.where(exists[1], 1, 0) + jnp.where(exists[-1], 1, 0)
    first, last = (lon == 0) & (lons > 2), (lon == lons - 1) & (lons > 2)
    expected = jnp.where(last, 0, in_column)
    for side in (-1, 1):
        greets, greeted = greetings(side)
        expected = expected + jnp.where(greeted, in_column + 1, 0)
        for north in (0, 1, -1):

            @pl.when(greets & exists[north])
            def _():
                pl.semaphore_signal(barrier, inc=1, device_id=neighbour(north, side), device_id_type=MESH)

    for north in (1, -1):

        @pl.when(exists[north] & ~last)
        def _():
            pl.semaphore_signal(barrier, inc=1, device_id=neighbour(north, 0), device_id_type=MESH)

    for north, rows in ((1, slice(8, 12)), (-1, slice(12, 16))):

        @pl.when(~exists[north])
        def _():
            west[:, rows, :] = jnp.zeros((2, 4, 128), jnp.float32)
            east[:, rows, :] = jnp.zeros((2, 4, 128), jnp.float32)
            ext[:, rows.start + 8 : rows.stop + 8, :] = jnp.zeros((PLANES, 4, 128), jnp.float32)

    west[:, 11:13, :] = jnp.zeros((2, 2, 128), jnp.float32)
    east[:, 11:13, :] = jnp.zeros((2, 2, 128), jnp.float32)
    plan = (
        (1, 1, packed.at[0:2, 5:8, :], west.at[:, 13:16, :]),
        (0, 1, packed.at[0:2], west.at[:, 0:8, :]),
        (-1, 1, packed.at[0:2, 0:3, :], west.at[:, 8:11, :]),
        (0, -1, packed.at[2:4], east.at[:, 0:8, :]),
        (1, -1, packed.at[2:4, 5:8, :], east.at[:, 13:16, :]),
        (-1, -1, packed.at[2:4, 0:3, :], east.at[:, 8:11, :]),
        (1, 0, ext.at[:, 12:16, :], ext.at[:, 20:24, :]),
        (-1, 0, ext.at[:, 8:12, :], ext.at[:, 16:20, :]),
    )
    copies = []
    for north, easterly, source, target in plan:
        copy = pltpu.make_async_remote_copy(
            src_ref=source,
            dst_ref=target,
            send_sem=send_sem.at[len(copies)],
            recv_sem=recv_sem.at[len(copies)],
            device_id=neighbour(north, easterly),
            device_id_type=MESH,
        )
        copies.append((copy, exists[north], exists[-north]))

    def start(chosen, condition):
        for copy, sent, _ in chosen:
            pl.when(sent & condition)(copy.start)

    def wait_recv(chosen):
        for copy, _, received in chosen:
            pl.when(received)(copy.wait_recv)

    def answer(side, theirs):
        for north in (0, 1, -1):

            @pl.when(~greetings(side)[0] & exists[north])
            def _():
                pl.semaphore_signal(theirs, inc=1, device_id=neighbour(north, side), device_id_type=MESH)

    eastward, westward, along = copies[0:3], copies[3:6], copies[6:8]
    pl.semaphore_wait(barrier, expected)
    answer(1, answer_sem.at[0])
    for load in loads:
        load.wait()
    ext[COUNT, 8:16, :] = jnp.where(mask[...] == 1, count[...], 0).astype(jnp.float32)
    pack_last(ext, packed)
    start(eastward, lon >= 0)
    pack_first(ext, packed)
    greeted = greetings(-1)[1]
    start(westward, greeted)
    start(along, ~last)

    def start_answered(condition):
        @pl.when(condition)
        def _():
            pl.semaphore_wait(answer_sem.at[0], in_column + 1)

        @pl.when(condition & first)
        def _():
            pl.semaphore_signal(told_sem, inc=1, device_id=neighbour(0, -1), device_id_type=MESH)

        start(westward, condition)

    @pl.when(last)
    def _():
        pl.semaphore_wait(told_sem, 1)

    start(along, last)
    start_answered(~greeted & last)
    wait_recv(along)
    interior(ext, adj_tracers, adj_east, adj_north, coefs, opens, states, sums)
    pack_strips(ext, own)
    for field in range(STRIPS):
        own_west[field] = turn(own[field], -4)
    wait_recv(westward)
    eastern_strip(own, east, adj_tracers, adj_east, adj_north)
    start_answered(~greeted & first)
    for copy, sent, _ in copies:
        pl.when(sent)(copy.wait_send)
    wait_recv(eastward)


def interior(ext, adj_tracers, adj_east, adj_north, coefs, opens, states, sums):
    ext[COUNT, 7:8, :] = ext[COUNT, 23:24, :]
    ext[COUNT, 24:25, :] = ext[COUNT, 8:9, :]

    def each_level(body):
        def step(level, carry):
            body(level)
            return carry

        lax.fori_loop(0, LEVELS, step, 0, unroll=UNROLL)

    def repeat_ends(level):
        for field in range(8):
            ext[8 * field + level, 7:8, :] = ext[8 * field + level, 23:24, :]
            ext[8 * field + level, 24:25, :] = ext[8 * field + level, 8:9, :]

    each_level(repeat_ends)

    def coefficients(level):
        here = level.astype(jnp.float32)
        cnt = ext[COUNT, 8:24, :]
        vel_e = ext[EAST + level, 8:24, :]
        open_e = jnp.minimum(cnt, turn(cnt, -1)) > here
        open_n = jnp.minimum(cnt, ext[COUNT, 9:25, :]) > here
        made = stencil(
            cnt > here,
            jnp.where(cnt > here + 1.0, VERT, 0.0),
            jnp.where(cnt > here, jnp.where(level > 0, VERT, 0.0), 0.0),
            vel_e,
            turn(vel_e, 1),
            ext[NORTH + level, 8:24, :],
            ext[NORTH + level, 7:23, :],
            open_e,
            jnp.minimum(cnt, turn(cnt, 1)) > here,
            open_n,
            jnp.minimum(cnt, ext[COUNT, 7:23, :]) > here,
        )
        for place, value in enumerate(made):
            coefs[level, place] = value
        opens[level, 0] = jnp.where(open_e[0:8], 0.5, 0.0)
        opens[level, 1] = jnp.where(open_n[0:8], 0.5, 0.0)

    each_level(coefficients)

    def near(source, origin, tracer, level, rows):
        base = origin + LEVELS * tracer
        value = source[base + level, 8 : 8 + rows, :]
        north, south = source[base + level, 9 : 9 + rows, :], source[base + level, 7 : 7 + rows, :]
        above = source[base + jnp.minimum(level + 1, LEVELS - 1), 8 : 8 + rows, :]
        below = source[base + jnp.maximum(level - 1, 0), 8 : 8 + rows, :]
        return value, turn(value, -1), turn(value, 1), north, south, above, below

    def forward_step(step, level):
        source = ext if step == 0 else states
        origin = TRACER if step == 0 else 24 * (step - 1)
        d, e, w, n, s, up, down = (coefs[level, name] for name in FORWARD)
        for tracer in range(TRACERS):
            value, after, before, north, south, above, below = near(source, origin, tracer, level, 16)
            result = d * value - e * after + w * before - n * north + s * south + up * above + down * below
            close_ring(states, 24 * step + LEVELS * tracer + level, result)
            sums[step, 0, LEVELS * tracer + level] = value[:8] + after[:8]
            sums[step, 1, LEVELS * tracer + level] = value[:8] + north[:8]

    def last_sums(level):
        for tracer in range(TRACERS):
            slab = 48 + LEVELS * tracer + level
            value = states[slab, 8:16, :]
            sums[3, 0, LEVELS * tracer + level] = value + turn(value, -1)
            sums[3, 1, LEVELS * tracer + level] = value + states[slab, 9:17, :]

    def adjoint_step(step, level):
        source = ext if step == 0 else states
        origin = COTAN if step == 0 else 24 * (step - 1)
        rows = 16 if step < 3 else 8
        d, e, w, n, s, up, down = (coefs[level, name, :rows] for name in ADJOINT)
        grad_e = jnp.zeros((8, 128), jnp.float32)
        grad_n = jnp.zeros((8, 128), jnp.float32)
        for tracer in range(TRACERS):
            value, after, before, north, south, above, below = near(source, origin, tracer, level, rows)
            result = d * value + e * after - w * before + n * north - s * south + up * above + down * below
            if step < 3:
                close_ring(states, 24 * step + LEVELS * tracer + level, result)
            else:
                adj_tracers[LEVELS * tracer + level] = result
            grad_e = grad_e + sums[3 - step, 0, LEVELS * tracer + level] * (after[:8] - value[:8])
            grad_n = grad_n + sums[3 - step, 1, LEVELS * tracer + level] * (north[:8] - value[:8])
        if step > 0:
            grad_e = grad_e + adj_east[level]
            grad_n = grad_n + adj_north[level]
        if step == 3:
            grad_e = grad_e * opens[level, 0]
            grad_n = grad_n * opens[level, 1]
        adj_east[level] = grad_e
        adj_north[level] = grad_n

    for step in range(3):
        each_level(lambda level, step=step: forward_step(step, level))
    each_level(last_sums)
    for step in range(4):
        each_level(lambda level, step=step: adjoint_step(step, level))


def western_kernel(part_tracers, part_east, part_north, own, west, adj_tracers, adj_east, adj_north):
    lane = lanes_of(16)
    place = lane % 16
    outer = place < 4
    odd = lane % 32 >= 16
    count = own[8]
    for half in range(2):
        for column, field in enumerate(SPARE):
            here = (place == column) & (odd if half else ~odd)
            count = jnp.where(here, turn(west[half], 16 * half + column - HALO * field), count)
    fields = []
    for field in range(8):
        arrived = jnp.where(odd, turn(west[1], 16 - HALO * field), turn(west[0], -HALO * field))
        fields.append(jnp.where(outer, arrived, own[field]))
    parts, targets = (part_tracers, part_east, part_north), (adj_tracers, adj_east, adj_north)
    patch(run_strip(fields, count), parts, targets, -4, lanes_of(8) < 4)


def on_device(tracers, cotangent, east_vel, north_vel, sea_mask, level_count):
    f32 = jnp.float32
    vmem = pl.BlockSpec(memory_space=pltpu.VMEM)
    operands = (tracers.reshape(24, 8, 128), cotangent.reshape(24, 8, 128), east_vel, north_vel, sea_mask, level_count)
    results = (
        jax.ShapeDtypeStruct((24, 8, 128), f32),
        jax.ShapeDtypeStruct((8, 8, 128), f32),
        jax.ShapeDtypeStruct((8, 8, 128), f32),
    )
    parts = pl.pallas_call(
        exchange_kernel,
        name="exchange",
        out_shape=(
            *results,
            jax.ShapeDtypeStruct((STRIPS, 16, 128), f32),
            jax.ShapeDtypeStruct((2, 16, 128), f32),
        ),
        in_specs=[pl.BlockSpec(memory_space=pltpu.HBM)] * 6,
        out_specs=(vmem,) * 5,
        scratch_shapes=[
            pltpu.VMEM((PLANES, ROWS, 128), f32),
            pltpu.VMEM((STRIPS, 16, 128), f32),
            pltpu.VMEM((2, 16, 128), f32),
            pltpu.VMEM((4, 8, 128), f32),
            pltpu.VMEM((8, 128), jnp.int32),
            pltpu.VMEM((8, 128), jnp.int32),
            pltpu.VMEM((LEVELS, 11, 16, 128), f32),
            pltpu.VMEM((LEVELS, 2, 8, 128), f32),
            pltpu.VMEM((72, ROWS, 128), f32),
            pltpu.VMEM((4, 2, 24, 8, 128), f32),
            pltpu.SemaphoreType.DMA((10,)),
            pltpu.SemaphoreType.DMA((8,)),
            pltpu.SemaphoreType.DMA((8,)),
            pltpu.SemaphoreType.REGULAR((1,)),
            pltpu.SemaphoreType.REGULAR,
        ],
        compiler_params=pltpu.CompilerParams(collective_id=0, has_side_effects=True, vmem_limit_bytes=16 << 20),
    )(*(pltpu.with_memory_space_constraint(operand, pltpu.HBM) for operand in operands))
    adj_tracers, adj_east, adj_north = pl.pallas_call(
        western_kernel,
        name="western",
        out_shape=results,
        in_specs=[vmem] * 5,
        out_specs=(vmem,) * 3,
        compiler_params=pltpu.CompilerParams(vmem_limit_bytes=16 << 20),
    )(*parts)
    return adj_tracers.reshape(tracers.shape), adj_east, adj_north


def solution(mesh):
    placed = (
        P(None, None, "lat", "lon"),
        P(None, None, "lat", "lon"),
        P(None, "lat", "lon"),
        P(None, "lat", "lon"),
        P("lat", "lon"),
        P("lat", "lon"),
    )
    return jax.shard_map(
        on_device,
        mesh=mesh,
        in_specs=placed,
        out_specs=(P(None, None, "lat", "lon"), P(None, "lat", "lon"), P(None, "lat", "lon")),
        check_vma=False,
    )
```
